32 devices in a mesh: group: 2 (over x), seq: 4 (over y, core), tp: 4 (over z).
Axes of the slice: x: 2, y: 2, z: 4, core: 2. Of those that a mesh axis runs over, the one named last changes fastest.
Arguments:
- queries: bfloat16 [4096, 4096], P(('group', 'seq'), 'tp'), parts along dimension 0, may hold values from -32 to 32
- key_value: bfloat16 [4096, 2, 2048], P(('group', 'seq'), None, 'tp'), parts along dimension 0, may hold values from -32 to 32
- window_cache: bfloat16 [2048, 2, 2048], P('group', None, 'tp'), parts along dimension 0, may hold values from -5 to 5
- span_start: int32 [2], P('group'), parts along dimension 0, may hold values from 1024 to 30720
- hidden: bfloat16 [4096, 21504], P(('group', 'seq'), 'tp'), parts along dimension 0, may hold values from -6 to 6
- down_codes: int32 [21504, 2688], P('tp', 'seq'), may hold values from 0 to 15
- down_scales: int32 [168, 2688], P('tp', 'seq'), may hold values from 1 to 15
- out_weight: bfloat16 [4096, 2688], P('tp', 'seq'), may hold values from -0.375 to 0.375
Outputs:
- layer_update: bfloat16 [4096, 2688], P(('group', 'seq', 'tp')), parts along dimension 0
The draws below stay inside these ranges and needn't reach their ends.
There are 2 independent parts, one for each index of `group`. The reference program is written for one: setup_inputs(seed, part) draws one part's arguments, and reference() takes and returns one part's arrays. A program takes and returns all parts, laid end to end along the dimension named above; an argument that names none is the same for every part. Nothing has to cross between parts.
All inputs are finite; a program needn't handle non-finite values.
Results may differ from the reference program's by a relative error of at most 0.02.
Values may be sent and summed in bfloat16 or wider, within the bound.
No kernel may reach another device: no remote copies, remote signals or barrier semaphores. Data moves between devices by JAX's collectives and lax.ppermute only.
A program may use at most 192 MiB of HBM per device.

```python
import jax
import jax.numpy as jnp
import numpy as np
from jax import lax

FF = 21504
HEADS = 32
KV_HEADS = 16
HD = 128
WINDOW = 1024
DW = 2688
GROUP = 128
TOKENS = 2048


def joint_draw(key):
    base = jax.random.fold_in(key, 1009)
    keys_split = jax.random.split(base, 2)
    wide_query = HEADS * HD
    wide_pair = KV_HEADS * HD
    query_rows = jax.random.truncated_normal(keys_split[0], -4.0, 4.0, (TOKENS, wide_query), jnp.float32)
    pair_rows = jax.random.truncated_normal(keys_split[1], -4.0, 4.0, (TOKENS, 2, wide_pair), jnp.float32)
    return (query_rows, pair_rows)


def draw_queries(key, part):
    return joint_draw(key)[0].astype(jnp.bfloat16)


def draw_key_value(key, part):
    return joint_draw(key)[1].astype(jnp.bfloat16)


def plant(drawn, rng, smallest, top_value):
    place = [jax.random.randint(jax.random.fold_in(rng, axis), (), 0, length) for axis, length in enumerate(drawn.shape)]
    longest = drawn.shape.index(max(drawn.shape))
    next_to = place[:longest] + [(place[longest] + 1) % drawn.shape[longest]] + place[longest + 1:]
    return drawn.at[tuple(place)].set(smallest).at[tuple(next_to)].set(top_value)


def level_of(key, dims, cuts, least, largest):
    loudness = 1.0
    for position, blocks in cuts:
        draws = jax.random.uniform(jax.random.fold_in(jax.random.fold_in(key, 6), position), (blocks,), jnp.float32, least / len(cuts), largest / len(cuts))
        loudness = loudness * jnp.repeat(jnp.exp(draws), dims[position] // blocks).reshape((-1,) + (1,) * (len(dims) - 1 - position))
    return loudness


def centred(stream_key, dims, spread, limit, cuts=(), held_as=jnp.bfloat16):
    values = jax.random.normal(stream_key, dims, jnp.float32) * spread
    if len(cuts) > 0:
        values = level_of(stream_key, dims, cuts, -0.22, 0.18) * values
    return jnp.clip(values, min=-limit, max=limit).astype(held_as)


def setup_inputs(seed: int = 0, part: int = 0) -> dict:
    streams_of = jax.random.split(jax.random.key(seed), 9)
    own_keys = jax.random.split(jax.random.fold_in(streams_of[8], part), 9)
    return {
        "queries": draw_queries(jax.random.fold_in(jax.random.fold_in(streams_of[8], part), 71), part),
        "key_value": draw_key_value(jax.random.fold_in(jax.random.fold_in(streams_of[8], part), 71), part),
        "window_cache": centred(own_keys[2], (WINDOW, 2, KV_HEADS * HD), 1.0, 5.0, ((2, 4),)),
        "span_start": jax.random.randint(own_keys[3], (1,), WINDOW, 32768 - TOKENS + 1).astype(jnp.int32),
        "hidden": centred(own_keys[4], (TOKENS, FF), 1.0, 6.0, ((0, 4), (1, 4))),
        "down_codes": plant(jax.random.randint(streams_of[5], (FF, DW), 0, 16), jax.random.fold_in(streams_of[5], 1), 0, 15).astype(jnp.int32),
        "down_scales": plant(jax.random.randint(streams_of[6], (FF // GROUP, DW), 1, 16), jax.random.fold_in(streams_of[6], 1), 1, 15).astype(jnp.int32),
        "out_weight": centred(streams_of[7], (HEADS * HD, DW), (HEADS * HD // 16) ** -0.5, 0.375, ((0, 4), (1, 4))),
    }


ROPE_BASE = 10000.0
SCORE_SCALE = 168.0 ** -0.5
CODE_STEP = 2.0 ** -14
INV_ROOT = 1344.0 ** -0.5


def bit_total(value_now):
    return (value_now & 1) + ((value_now >> 1) & 1) + ((value_now >> 2) & 1)


def build_tables():
    prime_order = 167
    residues = set((value_now * value_now) % prime_order for value_now in range(1, prime_order))
    legendre = [0] + [1 if value_now in residues else -1 for value_now in range(1, prime_order)]
    paley_table = np.eye(prime_order + 1)
    paley_table[0, 1:] += 1.0
    paley_table[1:, 0] -= 1.0
    for row_index in range(prime_order):
        for col_index in range(prime_order):
            paley_table[row_index + 1, col_index + 1] += legendre[(col_index - row_index) % prime_order]
    sylvester = np.array([[(-1.0) ** bit_total(left_bit & right_bit) for right_bit in range(8)] for left_bit in range(8)])
    return paley_table, sylvester


def rotary(values, cosine, sine_part):
    half_dim = values.shape[-1] // 2
    first_half = values[..., :half_dim]
    second_half = values[..., half_dim:]
    return jnp.concatenate([first_half * cosine - second_half * sine_part, second_half * cosine + first_half * sine_part], axis=-1)


def section_pairs(blocks_now, section_level):
    row_count, block_count, width_cols = blocks_now.shape
    paired = blocks_now.reshape(row_count, block_count >> (section_level + 1), 2, 1 << section_level, width_cols).astype(jnp.float32)
    upper_half = paired[:, :, 0]
    lower_half = paired[:, :, 1]
    mixed = jnp.stack([upper_half + lower_half, upper_half - lower_half], axis=2)
    return mixed.astype(jnp.bfloat16).reshape(row_count, block_count, width_cols)


def rotate_hidden(block_rows, paley_table, sylvester):
    row_count = block_rows.shape[0]
    parts_now = block_rows.astype(jnp.float32).reshape(row_count, 16, 8, 168)
    mixed = jnp.einsum("nbac,cd->nbad", parts_now, paley_table, precision=lax.Precision.HIGHEST)
    mixed = jnp.einsum("nbad,ae->nbed", mixed, sylvester, precision=lax.Precision.HIGHEST) * INV_ROOT
    blocks_now = mixed.reshape(row_count, 16, 1344).astype(jnp.bfloat16)
    for section_level in range(4):
        blocks_now = section_pairs(blocks_now, section_level)
    return blocks_now.reshape(row_count, 16 * 1344)


def reference(queries, key_value, window_cache, span_start, hidden, down_codes, down_scales, out_weight):
    first_pos = span_start[0]
    positions = (first_pos + jnp.arange(TOKENS, dtype=jnp.int32)).astype(jnp.float32)
    inv_freq = ROPE_BASE ** (-(2.0 * jnp.arange(HD // 2, dtype=jnp.float32)) / HD)
    angles = positions[:, None] * inv_freq[None, :]
    cosine = jnp.cos(angles)[:, None, :]
    sine_part = jnp.sin(angles)[:, None, :]
    query_rot = rotary(queries.astype(jnp.float32).reshape(TOKENS, HEADS, HD), cosine, sine_part).astype(jnp.bfloat16)
    key_rot = rotary(key_value[:, 0].astype(jnp.float32).reshape(TOKENS, KV_HEADS, HD), cosine, sine_part).astype(jnp.bfloat16)
    cycle_index = ((jnp.arange(WINDOW, dtype=jnp.int32) + first_pos % WINDOW) % WINDOW).astype(jnp.int32)
    ordered = jnp.take(window_cache, cycle_index, axis=0)
    all_keys = jnp.concatenate([ordered[:, 0].reshape(WINDOW, KV_HEADS, HD), key_rot], axis=0)
    all_values = jnp.concatenate([ordered[:, 1].reshape(WINDOW, KV_HEADS, HD), key_value[:, 1].reshape(TOKENS, KV_HEADS, HD)], axis=0)
    group_size = HEADS // KV_HEADS
    query_block = min(TOKENS, 512)

    def attend(block_first):
        grouped = lax.dynamic_slice_in_dim(query_rot, block_first, query_block, 0).astype(jnp.float32)
        grouped = grouped.reshape(query_block, KV_HEADS, group_size, HD)
        key_rows = lax.dynamic_slice_in_dim(all_keys, block_first, query_block + WINDOW, 0).astype(jnp.float32)
        value_rows = lax.dynamic_slice_in_dim(all_values, block_first, query_block + WINDOW, 0).astype(jnp.float32)
        scores = jnp.einsum("qkgd,skd->kgqs", grouped, key_rows) * SCORE_SCALE
        query_ids = jnp.arange(query_block)[:, None]
        key_ids = jnp.arange(query_block + WINDOW)[None, :]
        allowed = (key_ids > query_ids) & (key_ids <= query_ids + WINDOW)
        scores = jnp.where(allowed, scores, -jnp.inf)
        top_score = jnp.max(scores, axis=-1, keepdims=True)
        weights_soft = jnp.exp(scores - top_score)
        weights_soft = (weights_soft / jnp.sum(weights_soft, axis=-1, keepdims=True)).astype(jnp.bfloat16)
        attended = jnp.einsum("kgqs,skd->qkgd", weights_soft.astype(jnp.float32), value_rows)
        return attended.astype(jnp.bfloat16).reshape(query_block, HEADS * HD)

    block_starts = (jnp.arange(TOKENS // query_block, dtype=jnp.int32) * query_block).astype(jnp.int32)
    attn = lax.map(attend, block_starts).reshape(TOKENS, HEADS * HD)

    scale_rows = jnp.repeat(down_scales, GROUP, axis=0)
    down_weight = ((down_codes - 8) * scale_rows).astype(jnp.float32) * CODE_STEP
    weights_all = jnp.concatenate([down_weight.astype(jnp.bfloat16), out_weight], axis=0)
    paley_np, sylvester_np = build_tables()
    paley_table = jnp.asarray(paley_np, dtype=jnp.float32)
    sylvester = jnp.asarray(sylvester_np, dtype=jnp.float32)
    ffn_block = min(TOKENS, 1024)

    def project(block_first):
        block_rows = lax.dynamic_slice_in_dim(hidden, block_first, ffn_block, 0)
        side_rows = lax.dynamic_slice_in_dim(attn, block_first, ffn_block, 0)
        joined = jnp.concatenate([rotate_hidden(block_rows, paley_table, sylvester), side_rows], axis=1)
        return jnp.dot(joined, weights_all, preferred_element_type=jnp.float32).astype(jnp.bfloat16)

    ffn_starts = (jnp.arange(TOKENS // ffn_block, dtype=jnp.int32) * ffn_block).astype(jnp.int32)
    return lax.map(project, ffn_starts).reshape(TOKENS, DW)
```

```python
import jax
import jax.numpy as jnp
import numpy as np
from jax import lax
from jax.experimental import pallas as pl
from jax.experimental.pallas import tpu as pltpu
from jax.sharding import PartitionSpec as P

HD = 128
WINDOW = 1024
GROUP = 128


ROPE_BASE = 10000.0
SCORE_SCALE = 168.0 ** (-0.5)
CODE_STEP = 2.0 ** (-14)
INV_ROOT = 1344.0 ** (-0.5)


def shifted(value, axis, steps):
    count = lax.axis_size(axis)
    first, last = (max(0, -steps), min(count, count - steps))
    return lax.ppermute(value, axis, [(source, source + steps) for source in range(first, last)])


def swapped(x, axis, stride):
    return lax.ppermute(x, axis, [(i, i ^ 1 << stride) for i in range(lax.axis_size(axis))])


def bit_total(value_now):
    return (value_now & 1) + (value_now >> 1 & 1) + (value_now >> 2 & 1)


def build_tables():
    prime_order = 167
    residues = set((value_now * value_now % prime_order for value_now in range(1, prime_order)))
    legendre = [0] + [1 if value_now in residues else -1 for value_now in range(1, prime_order)]
    paley_table = np.eye(prime_order + 1)
    paley_table[0, 1:] += 1.0
    paley_table[1:, 0] -= 1.0
    for row_index in range(prime_order):
        for col_index in range(prime_order):
            paley_table[row_index + 1, col_index + 1] += legendre[
                (col_index - row_index) % prime_order
            ]
    sylvester = np.array(
        [
            [(-1.0) ** bit_total(left_bit & right_bit) for right_bit in range(8)]
            for left_bit in range(8)
        ]
    )
    return (paley_table, sylvester)


def rotary(values, cosine, sine_part):
    half_dim = values.shape[-1] // 2
    first_half = values[..., :half_dim]
    second_half = values[..., half_dim:]
    return jnp.concatenate(
        [
            first_half * cosine - second_half * sine_part,
            second_half * cosine + first_half * sine_part,
        ],
        axis=-1,
    )


def section_pairs(blocks_now, section_level):
    row_count, block_count, width_cols = blocks_now.shape
    paired = blocks_now.reshape(
        row_count, block_count >> section_level + 1, 2, 1 << section_level, width_cols
    ).astype(jnp.float32)
    upper_half = paired[:, :, 0]
    lower_half = paired[:, :, 1]
    mixed = jnp.stack([upper_half + lower_half, upper_half - lower_half], axis=2)
    return mixed.astype(jnp.bfloat16).reshape(row_count, block_count, width_cols)


def per_device(
    queries, key_value, window_cache, span_start, hidden, down_codes, down_scales, out_weight
):
    tok_rows = queries.shape[0]
    tp_count = lax.axis_size("tp")
    seq_index = lax.axis_index("seq")
    tp_index = lax.axis_index("tp")
    heads_dev = queries.shape[1] // HD
    kv_dev = key_value.shape[2] // HD
    group_size = heads_dev // kv_dev
    first_pos = span_start[0]
    positions = first_pos + seq_index * tok_rows + jnp.arange(tok_rows, dtype=jnp.int32)
    inv_freq = ROPE_BASE ** (-(2.0 * jnp.arange(HD // 2, dtype=jnp.float32)) / HD)
    angles = positions.astype(jnp.float32)[:, None] * inv_freq[None, :]
    cosine = jnp.cos(angles)[:, None, :]
    sine_part = jnp.sin(angles)[:, None, :]
    query_rot = rotary(
        queries.reshape(tok_rows, heads_dev, HD).astype(jnp.float32), cosine, sine_part
    ).astype(jnp.bfloat16)
    key_rot = rotary(
        key_value[:, 0].reshape(tok_rows, kv_dev, HD).astype(jnp.float32), cosine, sine_part
    ).astype(jnp.bfloat16)
    own_pairs = jnp.stack([key_rot.reshape(tok_rows, kv_dev * HD), key_value[:, 1]], axis=1)
    reach_blocks = WINDOW // tok_rows
    earlier = []
    moving = own_pairs
    for hop_count in range(reach_blocks):
        moving = shifted(moving, "seq", 1)
        earlier.insert(0, moving)
    halo_rows = jnp.concatenate(earlier, axis=0)
    doubled = jnp.concatenate([window_cache, window_cache], axis=0)
    ordered = lax.dynamic_slice_in_dim(doubled, first_pos % WINDOW, WINDOW, 0)
    padded_cache = jnp.concatenate([ordered, jnp.zeros_like(ordered)], axis=0)
    from_cache = lax.dynamic_slice_in_dim(
        padded_cache, jnp.minimum(seq_index * tok_rows, WINDOW), WINDOW, 0
    )
    halo_rows = halo_rows + from_cache
    all_rows = jnp.concatenate([halo_rows, own_pairs], axis=0)
    key_count = all_rows.shape[0]
    key_rows = all_rows[:, 0].reshape(key_count, kv_dev, HD)
    value_rows = all_rows[:, 1].reshape(key_count, kv_dev, HD)
    grouped = query_rot.reshape(tok_rows, kv_dev, group_size, HD)
    scores = (
        jnp.einsum("qkgd,skd->kgqs", grouped, key_rows, preferred_element_type=jnp.float32)
        * SCORE_SCALE
    )
    query_ids = jnp.arange(tok_rows)[:, None]
    key_ids = jnp.arange(key_count)[None, :]
    allowed = (key_ids > query_ids) & (key_ids <= query_ids + WINDOW)
    scores = jnp.where(allowed, scores, -jnp.inf)
    top_score = jnp.max(scores, axis=-1, keepdims=True)
    weights_soft = jnp.exp(scores - top_score)
    weights_soft = (weights_soft / jnp.sum(weights_soft, axis=-1, keepdims=True)).astype(
        jnp.bfloat16
    )
    attended = jnp.einsum(
        "kgqs,skd->qkgd", weights_soft, value_rows, preferred_element_type=jnp.float32
    )
    attended = attended.astype(jnp.bfloat16).reshape(tok_rows, heads_dev * HD)
    paley_np, sylvester_np = build_tables()
    paley_table = jnp.asarray(paley_np, dtype=jnp.bfloat16)
    sylvester = jnp.asarray(sylvester_np, dtype=jnp.float32)
    local_blocks = hidden.shape[1] // 1344
    local_levels = local_blocks.bit_length() - 1
    parts_now = hidden.reshape(tok_rows, local_blocks, 8, 168)
    mixed = jnp.einsum("nbac,cd->nbad", parts_now, paley_table, preferred_element_type=jnp.float32)
    mixed = (
        jnp.einsum("nbad,ae->nbed", mixed, sylvester, precision=lax.Precision.HIGHEST) * INV_ROOT
    )
    blocks_now = mixed.reshape(tok_rows, local_blocks, 1344).astype(jnp.bfloat16)
    for section_level in range(local_levels):
        blocks_now = section_pairs(blocks_now, section_level)
    for bit_index in range(tp_count.bit_length() - 1):
        partner = swapped(blocks_now, "tp", bit_index)
        high_side = jnp.right_shift(tp_index, bit_index) % 2
        own_values = blocks_now.astype(jnp.float32)
        other_values = partner.astype(jnp.float32)
        blocks_now = jnp.where(
            high_side == 0, own_values + other_values, other_values - own_values
        ).astype(jnp.bfloat16)
    rotated = blocks_now.reshape(tok_rows, local_blocks * 1344)
    joined = jnp.concatenate([rotated, attended], axis=1)
    group_count = down_scales.shape[0]
    col_count = down_codes.shape[1]
    down_weight = (
        (down_codes.reshape(group_count, GROUP, col_count) - 8) * down_scales[:, None, :]
    ).astype(jnp.float32) * CODE_STEP
    down_rows = down_weight.astype(jnp.bfloat16).reshape(group_count * GROUP, col_count)
    stacked = jnp.concatenate([down_rows, out_weight], axis=0)
    partials = jnp.dot(
        joined,
        lax.all_gather(stacked, "seq", axis=1, tiled=True),
        preferred_element_type=jnp.float32,
    )
    layer_update = lax.psum_scatter(
        partials.astype(jnp.bfloat16), "tp", scatter_dimension=0, tiled=True
    )
    return layer_update


BLOCK = 1344
PADDED = 1408


def fits(mesh):
    return dict(mesh.shape) == {"group": 2, "seq": 4, "tp": 4}


def mix_tables():
    paley_np, sylvester_np = build_tables()
    mix_np = np.kron(sylvester_np, paley_np)
    low = np.zeros((PADDED, PADDED), np.float32)
    high = np.zeros((PADDED, PADDED), np.float32)
    low[:BLOCK, :BLOCK] = mix_np
    high[PADDED - BLOCK :, :BLOCK] = mix_np
    return jnp.asarray(np.stack([low, high]), dtype=jnp.bfloat16)


def mix_kernel(hidden_ref, table_ref, out_ref):
    gap = PADDED - BLOCK
    pair = 2 * BLOCK

    def product(first, table):
        return jnp.dot(
            hidden_ref[:, first : first + PADDED],
            table_ref[table],
            preferred_element_type=jnp.float32,
        )

    sums, differences = [], []
    for half in range(2):
        even = product(half * pair, 0)
        odd = product(half * pair + BLOCK - gap, 1)
        sums.append(even + odd)
        differences.append(even - odd)
    for half in range(2):
        if half == 0:
            even, odd = sums[0] + sums[1], differences[0] + differences[1]
        else:
            even, odd = sums[0] - sums[1], differences[0] - differences[1]
        even, odd = even * INV_ROOT, pltpu.roll(odd * INV_ROOT, gap, 1)
        first, edge = half * pair, BLOCK - gap
        out_ref[:, first : first + edge] = even[:, :edge].astype(jnp.bfloat16)
        out_ref[:, first + edge : first + PADDED] = (even[:, edge:] + odd[:, : 2 * gap]).astype(
            jnp.bfloat16
        )
        out_ref[:, first + PADDED : first + pair] = odd[:, 2 * gap :].astype(jnp.bfloat16)


def mix_hidden(hidden):
    rows, width = hidden.shape
    step = 256
    return pl.pallas_call(
        mix_kernel,
        grid=(rows // step,),
        in_specs=[
            pl.BlockSpec((step, width), lambda i: (i, 0)),
            pl.BlockSpec((2, PADDED, PADDED), lambda i: (0, 0, 0)),
        ],
        out_specs=pl.BlockSpec((step, width), lambda i: (i, 0)),
        out_shape=jax.ShapeDtypeStruct((rows, width), jnp.bfloat16),
        compiler_params=pltpu.CompilerParams(vmem_limit_bytes=56 << 20),
        cost_estimate=pl.CostEstimate(
            flops=2 * rows * width * PADDED, bytes_accessed=4 * rows * width, transcendentals=0
        ),
    )(hidden, mix_tables())


CHUNKS = ((0, 256), (256, 256), (512, 160))


def dequant_kernel(half_ref, codes_ref, scales_ref, *out_refs):
    row = half_ref[0] * pl.num_programs(0) + pl.program_id(0)
    weight = ((codes_ref[...] - 8) * scales_ref[pl.ds(row, 1), :]).astype(jnp.float32) * CODE_STEP
    for (first, size), out_ref in zip(CHUNKS, out_refs):
        part = weight[:, first : first + size]
        extra = -size % 128
        if extra:
            part = jnp.concatenate([part, jnp.zeros((GROUP, extra), jnp.float32)], axis=1)
        out_ref[...] = part.T[:size].astype(jnp.bfloat16)


def dequant(half_id, codes, scales):
    rows, cols = codes.shape
    steps = rows // 2 // GROUP
    return pl.pallas_call(
        dequant_kernel,
        grid_spec=pltpu.PrefetchScalarGridSpec(
            num_scalar_prefetch=1,
            grid=(steps,),
            in_specs=[
                pl.BlockSpec((GROUP, cols), lambda i, half: (half[0] * steps + i, 0)),
                pl.BlockSpec(scales.shape, lambda i, half: (0, 0)),
            ],
            out_specs=[pl.BlockSpec((size, GROUP), lambda i, half: (0, i)) for _, size in CHUNKS],
        ),
        out_shape=[jax.ShapeDtypeStruct((size, rows // 2), jnp.bfloat16) for _, size in CHUNKS],
        cost_estimate=pl.CostEstimate(
            flops=2 * rows * cols, bytes_accessed=4 * rows * cols, transcendentals=0
        ),
    )(half_id, codes, scales)


NT = (((1,), (1,)), ((), ()))


def project_kernel(half_ref, *refs):
    (own_a, own_b, far_a, far_b, own_attn, far_attn) = refs[:6]
    weights = refs[6:12]
    out_ref = refs[12]
    size = weights[0].shape[0]
    rows_a = jnp.concatenate([own_a[...], far_a[...]], axis=0)
    rows_b = jnp.concatenate([own_b[...], far_b[...]], axis=0)
    rows_c = jnp.concatenate([own_attn[...], far_attn[...]], axis=0)
    for core in range(2):
        part_a, part_b, part_c = weights[3 * core : 3 * core + 3]
        total = lax.dot_general(rows_a, part_a[...], NT, preferred_element_type=jnp.float32)
        total += lax.dot_general(rows_b, part_b[...], NT, preferred_element_type=jnp.float32)
        total += jnp.dot(rows_c, part_c[...], preferred_element_type=jnp.float32)[:, :size]
        out_ref[core] = total.astype(jnp.bfloat16)


def project(half_id, own, far, own_attn, far_attn, weights, chunk):
    first, size = CHUNKS[chunk]
    rows, width = own.shape
    half = width // 2
    heads = own_attn.shape[1]
    step = rows // 4
    column = first // 256
    row_specs = [
        pl.BlockSpec((step, half), lambda i, h: (i, h[0])),
        pl.BlockSpec((step, half), lambda i, h: (i, 1 - h[0])),
    ]
    attn_spec = pl.BlockSpec((step, heads), lambda i, h: (i, 0))
    weight_spec = pl.BlockSpec((size, half), lambda i, h: (0, 0))
    side_spec = pl.BlockSpec((heads, 256), lambda i, h: (0, column))
    return pl.pallas_call(
        project_kernel,
        grid_spec=pltpu.PrefetchScalarGridSpec(
            num_scalar_prefetch=1,
            grid=(4,),
            in_specs=row_specs * 2 + [attn_spec] * 2 + [weight_spec, weight_spec, side_spec] * 2,
            out_specs=pl.BlockSpec((2, 2 * step, size), lambda i, h: (0, i, 0)),
        ),
        out_shape=jax.ShapeDtypeStruct((2, 2 * rows, size), jnp.bfloat16),
        compiler_params=pltpu.CompilerParams(vmem_limit_bytes=56 << 20),
        cost_estimate=pl.CostEstimate(
            flops=2 * 2 * rows * (width + heads) * 2 * size,
            bytes_accessed=2 * (2 * rows * (width + heads) + 2 * size * (width + heads)),
            transcendentals=0,
        ),
    )(half_id, own, own, far, far, own_attn, far_attn, *weights)


def attend(queries, key_value, window_cache, first_pos):
    tok_rows = queries.shape[0]
    seq_index = lax.axis_index("seq")
    heads_dev = queries.shape[1] // HD
    kv_dev = key_value.shape[2] // HD
    group_size = heads_dev // kv_dev
    positions = first_pos + seq_index * tok_rows + jnp.arange(tok_rows, dtype=jnp.int32)
    inv_freq = ROPE_BASE ** (-(2.0 * jnp.arange(HD // 2, dtype=jnp.float32)) / HD)
    angles = positions.astype(jnp.float32)[:, None] * inv_freq[None, :]
    cosine = jnp.cos(angles)[:, None, :]
    sine_part = jnp.sin(angles)[:, None, :]
    query_rot = rotary(
        queries.reshape(tok_rows, heads_dev, HD).astype(jnp.float32), cosine, sine_part
    ).astype(jnp.bfloat16)
    key_rot = rotary(
        key_value[:, 0].reshape(tok_rows, kv_dev, HD).astype(jnp.float32), cosine, sine_part
    ).astype(jnp.bfloat16)
    own_pairs = jnp.stack([key_rot.reshape(tok_rows, kv_dev * HD), key_value[:, 1]], axis=1)
    earlier = []
    moving = own_pairs
    for hop_count in range(WINDOW // tok_rows):
        moving = shifted(moving, "seq", 1)
        earlier.insert(0, moving)
    halo_rows = jnp.concatenate(earlier, axis=0)
    doubled = jnp.concatenate([window_cache, window_cache], axis=0)
    ordered = lax.dynamic_slice_in_dim(doubled, first_pos % WINDOW, WINDOW, 0)
    padded_cache = jnp.concatenate([ordered, jnp.zeros_like(ordered)], axis=0)
    from_cache = lax.dynamic_slice_in_dim(
        padded_cache, jnp.minimum(seq_index * tok_rows, WINDOW), WINDOW, 0
    )
    halo_rows = halo_rows + from_cache
    all_rows = jnp.concatenate([halo_rows, own_pairs], axis=0)
    key_count = all_rows.shape[0]
    key_rows = all_rows[:, 0].reshape(key_count, kv_dev, HD)
    value_rows = all_rows[:, 1].reshape(key_count, kv_dev, HD)
    grouped = query_rot.reshape(tok_rows, kv_dev, group_size, HD)
    scores = (
        jnp.einsum("qkgd,skd->kgqs", grouped, key_rows, preferred_element_type=jnp.float32)
        * SCORE_SCALE
    )
    query_ids = jnp.arange(tok_rows)[:, None]
    key_ids = jnp.arange(key_count)[None, :]
    allowed = (key_ids > query_ids) & (key_ids <= query_ids + WINDOW)
    scores = jnp.where(allowed, scores, -jnp.inf)
    top_score = jnp.max(scores, axis=-1, keepdims=True)
    weights_soft = jnp.exp(scores - top_score)
    weights_soft = (weights_soft / jnp.sum(weights_soft, axis=-1, keepdims=True)).astype(
        jnp.bfloat16
    )
    attended = jnp.einsum(
        "kgqs,skd->qkgd", weights_soft, value_rows, preferred_element_type=jnp.float32
    )
    return attended.astype(jnp.bfloat16).reshape(tok_rows, heads_dev * HD)


def flipped(value, axis, bit):
    return lax.ppermute(value, axis, [(i, i ^ bit) for i in range(lax.axis_size(axis))])


def level_step(value, bit):
    partner = flipped(value, "tp", bit).astype(jnp.float32)
    own = value.astype(jnp.float32)
    own = jnp.where(lax.axis_index("tp") & bit == 0, own, -own)
    return (own + partner).astype(jnp.bfloat16)


def planned(
    queries, key_value, window_cache, span_start, hidden, down_codes, down_scales, out_weight
):
    half_id = lax.axis_index("group").reshape(1)
    seq_index = lax.axis_index("seq")
    core = seq_index & 1
    side = seq_index >> 1
    chunks = dequant(half_id, down_codes, down_scales)
    rotated = mix_hidden(hidden)
    far_rotated = flipped(rotated, "seq", 2)
    attended = attend(queries, key_value, window_cache, span_start[0])
    far_attended = flipped(attended, "seq", 2)
    near_out = flipped(out_weight, "seq", 1)
    reduced = []
    for chunk, piece in enumerate(chunks):
        for bit in (2, 1) if chunk == 0 else (1, 2):
            piece = level_step(piece, bit)
        across = flipped(piece, "group", 1)
        near_piece = flipped(piece, "seq", 1)
        near_across = flipped(across, "seq", 1)
        partial = project(
            half_id,
            rotated,
            far_rotated,
            attended,
            far_attended,
            [piece, across, out_weight, near_piece, near_across, near_out],
            chunk,
        )
        reduced.append(lax.psum_scatter(partial, "tp", scatter_dimension=1, tiled=True))
    kept = queries.shape[0] // lax.axis_size("tp")
    own_side = jnp.concatenate([part[:, :kept] for part in reduced], axis=2)
    far_side = flipped(jnp.concatenate([part[:, kept:] for part in reduced], axis=2), "seq", 2)
    own_side = jnp.where(core == 0, own_side, own_side[::-1])
    far_side = jnp.where(core == 0, far_side, far_side[::-1])
    first = jnp.where(side == 0, own_side, far_side)
    second = jnp.where(side == 0, far_side, own_side)
    return jnp.concatenate([first[0], first[1], second[0], second[1]], axis=1)


def solution(mesh):
    return jax.shard_map(
        planned if fits(mesh) else per_device,
        mesh=mesh,
        in_specs=(
            P(("group", "seq"), "tp"),
            P(("group", "seq"), None, "tp"),
            P("group", None, "tp"),
            P("group"),
            P(("group", "seq"), "tp"),
            P("tp", "seq"),
            P("tp", "seq"),
            P("tp", "seq"),
        ),
        out_specs=P(("group", "seq", "tp"), None),
        check_vma=False,
    )
```

```python
import jax
import jax.numpy as jnp
import numpy as np
from jax import lax
from jax.experimental import pallas as pl
from jax.experimental.pallas import tpu as pltpu
from jax.sharding import PartitionSpec as P

HD = 128
WINDOW = 1024
GROUP = 128


ROPE_BASE = 10000.0
SCORE_SCALE = 168.0 ** (-0.5)
CODE_STEP = 2.0 ** (-14)
INV_ROOT = 1344.0 ** (-0.5)


def shifted(value, axis, steps):
    count = lax.axis_size(axis)
    first, last = (max(0, -steps), min(count, count - steps))
    return lax.ppermute(value, axis, [(source, source + steps) for source in range(first, last)])


def swapped(x, axis, stride):
    return lax.ppermute(x, axis, [(i, i ^ 1 << stride) for i in range(lax.axis_size(axis))])


def bit_total(value_now):
    return (value_now & 1) + (value_now >> 1 & 1) + (value_now >> 2 & 1)


def build_tables():
    prime_order = 167
    residues = set((value_now * value_now % prime_order for value_now in range(1, prime_order)))
    legendre = [0] + [1 if value_now in residues else -1 for value_now in range(1, prime_order)]
    paley_table = np.eye(prime_order + 1)
    paley_table[0, 1:] += 1.0
    paley_table[1:, 0] -= 1.0
    for row_index in range(prime_order):
        for col_index in range(prime_order):
            paley_table[row_index + 1, col_index + 1] += legendre[
                (col_index - row_index) % prime_order
            ]
    sylvester = np.array(
        [
            [(-1.0) ** bit_total(left_bit & right_bit) for right_bit in range(8)]
            for left_bit in range(8)
        ]
    )
    return (paley_table, sylvester)


def rotary(values, cosine, sine_part):
    half_dim = values.shape[-1] // 2
    first_half = values[..., :half_dim]
    second_half = values[..., half_dim:]
    return jnp.concatenate(
        [
            first_half * cosine - second_half * sine_part,
            second_half * cosine + first_half * sine_part,
        ],
        axis=-1,
    )


def section_pairs(blocks_now, section_level):
    row_count, block_count, width_cols = blocks_now.shape
    paired = blocks_now.reshape(
        row_count, block_count >> section_level + 1, 2, 1 << section_level, width_cols
    ).astype(jnp.float32)
    upper_half = paired[:, :, 0]
    lower_half = paired[:, :, 1]
    mixed = jnp.stack([upper_half + lower_half, upper_half - lower_half], axis=2)
    return mixed.astype(jnp.bfloat16).reshape(row_count, block_count, width_cols)


def per_device(
    queries, key_value, window_cache, span_start, hidden, down_codes, down_scales, out_weight
):
    tok_rows = queries.shape[0]
    tp_count = lax.axis_size("tp")
    seq_index = lax.axis_index("seq")
    tp_index = lax.axis_index("tp")
    heads_dev = queries.shape[1] // HD
    kv_dev = key_value.shape[2] // HD
    group_size = heads_dev // kv_dev
    first_pos = span_start[0]
    positions = first_pos + seq_index * tok_rows + jnp.arange(tok_rows, dtype=jnp.int32)
    inv_freq = ROPE_BASE ** (-(2.0 * jnp.arange(HD // 2, dtype=jnp.float32)) / HD)
    angles = positions.astype(jnp.float32)[:, None] * inv_freq[None, :]
    cosine = jnp.cos(angles)[:, None, :]
    sine_part = jnp.sin(angles)[:, None, :]
    query_rot = rotary(
        queries.reshape(tok_rows, heads_dev, HD).astype(jnp.float32), cosine, sine_part
    ).astype(jnp.bfloat16)
    key_rot = rotary(
        key_value[:, 0].reshape(tok_rows, kv_dev, HD).astype(jnp.float32), cosine, sine_part
    ).astype(jnp.bfloat16)
    own_pairs = jnp.stack([key_rot.reshape(tok_rows, kv_dev * HD), key_value[:, 1]], axis=1)
    reach_blocks = WINDOW // tok_rows
    earlier = []
    moving = own_pairs
    for hop_count in range(reach_blocks):
        moving = shifted(moving, "seq", 1)
        earlier.insert(0, moving)
    halo_rows = jnp.concatenate(earlier, axis=0)
    doubled = jnp.concatenate([window_cache, window_cache], axis=0)
    ordered = lax.dynamic_slice_in_dim(doubled, first_pos % WINDOW, WINDOW, 0)
    padded_cache = jnp.concatenate([ordered, jnp.zeros_like(ordered)], axis=0)
    from_cache = lax.dynamic_slice_in_dim(
        padded_cache, jnp.minimum(seq_index * tok_rows, WINDOW), WINDOW, 0
    )
    halo_rows = halo_rows + from_cache
    all_rows = jnp.concatenate([halo_rows, own_pairs], axis=0)
    key_count = all_rows.shape[0]
    key_rows = all_rows[:, 0].reshape(key_count, kv_dev, HD)
    value_rows = all_rows[:, 1].reshape(key_count, kv_dev, HD)
    grouped = query_rot.reshape(tok_rows, kv_dev, group_size, HD)
    scores = (
        jnp.einsum("qkgd,skd->kgqs", grouped, key_rows, preferred_element_type=jnp.float32)
        * SCORE_SCALE
    )
    query_ids = jnp.arange(tok_rows)[:, None]
    key_ids = jnp.arange(key_count)[None, :]
    allowed = (key_ids > query_ids) & (key_ids <= query_ids + WINDOW)
    scores = jnp.where(allowed, scores, -jnp.inf)
    top_score = jnp.max(scores, axis=-1, keepdims=True)
    weights_soft = jnp.exp(scores - top_score)
    weights_soft = (weights_soft / jnp.sum(weights_soft, axis=-1, keepdims=True)).astype(
        jnp.bfloat16
    )
    attended = jnp.einsum(
        "kgqs,skd->qkgd", weights_soft, value_rows, preferred_element_type=jnp.float32
    )
    attended = attended.astype(jnp.bfloat16).reshape(tok_rows, heads_dev * HD)
    paley_np, sylvester_np = build_tables()
    paley_table = jnp.asarray(paley_np, dtype=jnp.bfloat16)
    sylvester = jnp.asarray(sylvester_np, dtype=jnp.float32)
    local_blocks = hidden.shape[1] // 1344
    local_levels = local_blocks.bit_length() - 1
    parts_now = hidden.reshape(tok_rows, local_blocks, 8, 168)
    mixed = jnp.einsum("nbac,cd->nbad", parts_now, paley_table, preferred_element_type=jnp.float32)
    mixed = (
        jnp.einsum("nbad,ae->nbed", mixed, sylvester, precision=lax.Precision.HIGHEST) * INV_ROOT
    )
    blocks_now = mixed.reshape(tok_rows, local_blocks, 1344).astype(jnp.bfloat16)
    for section_level in range(local_levels):
        blocks_now = section_pairs(blocks_now, section_level)
    for bit_index in range(tp_count.bit_length() - 1):
        partner = swapped(blocks_now, "tp", bit_index)
        high_side = jnp.right_shift(tp_index, bit_index) % 2
        own_values = blocks_now.astype(jnp.float32)
        other_values = partner.astype(jnp.float32)
        blocks_now = jnp.where(
            high_side == 0, own_values + other_values, other_values - own_values
        ).astype(jnp.bfloat16)
    rotated = blocks_now.reshape(tok_rows, local_blocks * 1344)
    joined = jnp.concatenate([rotated, attended], axis=1)
    group_count = down_scales.shape[0]
    col_count = down_codes.shape[1]
    down_weight = (
        (down_codes.reshape(group_count, GROUP, col_count) - 8) * down_scales[:, None, :]
    ).astype(jnp.float32) * CODE_STEP
    down_rows = down_weight.astype(jnp.bfloat16).reshape(group_count * GROUP, col_count)
    stacked = jnp.concatenate([down_rows, out_weight], axis=0)
    partials = jnp.dot(
        joined,
        lax.all_gather(stacked, "seq", axis=1, tiled=True),
        preferred_element_type=jnp.float32,
    )
    layer_update = lax.psum_scatter(
        partials.astype(jnp.bfloat16), "tp", scatter_dimension=0, tiled=True
    )
    return layer_update


BLOCK = 1344
PADDED = 1408
CHUNKS = ((0, 256), (256, 256), (512, 160))
NT = (((1,), (1,)), ((), ()))
ANYWHERE = pl.BlockSpec(memory_space=pl.ANY)


def fits(mesh):
    return dict(mesh.shape) == {"group": 2, "seq": 4, "tp": 4}


def mix_tables():
    paley_np, sylvester_np = build_tables()
    mix_np = np.kron(sylvester_np, paley_np)
    low = np.zeros((PADDED, PADDED), np.float32)
    high = np.zeros((PADDED, PADDED), np.float32)
    low[:BLOCK, :BLOCK] = mix_np
    high[PADDED - BLOCK :, :BLOCK] = mix_np
    return jnp.asarray(np.stack([low, high]), dtype=jnp.bfloat16)


def mix_kernel(hidden_ref, table_ref, _, out_ref):
    gap = PADDED - BLOCK
    pair = 2 * BLOCK

    def product(first, table):
        return jnp.dot(
            hidden_ref[:, first : first + PADDED],
            table_ref[table],
            preferred_element_type=jnp.float32,
        )

    sums, differences = [], []
    for half in range(2):
        even = product(half * pair, 0)
        odd = product(half * pair + BLOCK - gap, 1)
        sums.append(even + odd)
        differences.append(even - odd)
    for half in range(2):
        if half == 0:
            even, odd = sums[0] + sums[1], differences[0] + differences[1]
        else:
            even, odd = sums[0] - sums[1], differences[0] - differences[1]
        even, odd = even * INV_ROOT, pltpu.roll(odd * INV_ROOT, gap, 1)
        first, edge = half * pair, BLOCK - gap
        out_ref[:, first : first + edge] = even[:, :edge].astype(jnp.bfloat16)
        out_ref[:, first + edge : first + PADDED] = (even[:, edge:] + odd[:, : 2 * gap]).astype(
            jnp.bfloat16
        )
        out_ref[:, first + PADDED : first + pair] = odd[:, 2 * gap :].astype(jnp.bfloat16)


def mix_hidden(hidden, earlier):
    rows, width = hidden.shape
    step = 256
    return pl.pallas_call(
        mix_kernel,
        grid=(rows // step,),
        in_specs=[
            pl.BlockSpec((step, width), lambda i: (i, 0)),
            pl.BlockSpec((2, PADDED, PADDED), lambda i: (0, 0, 0)),
            ANYWHERE,
        ],
        out_specs=pl.BlockSpec((step, width), lambda i: (i, 0)),
        out_shape=jax.ShapeDtypeStruct((rows, width), jnp.bfloat16),
        compiler_params=pltpu.CompilerParams(vmem_limit_bytes=56 << 20),
        cost_estimate=pl.CostEstimate(
            flops=2 * rows * width * PADDED, bytes_accessed=4 * rows * width, transcendentals=0
        ),
    )(hidden, mix_tables(), earlier)


def dequant_kernel(half_ref, codes_ref, scales_ref, *refs):
    out_ref = refs[-1]
    for group in range(codes_ref.shape[1] // GROUP):
        lanes = slice(group * GROUP, (group + 1) * GROUP)
        scale = scales_ref[:, group : group + 1] * CODE_STEP
        out_ref[:, lanes] = ((codes_ref[:, lanes] - 8).astype(jnp.float32) * scale).astype(
            jnp.bfloat16
        )


def dequant(half_id, codes, scales, chunk, earlier=()):
    width = codes.shape[1] // 2
    first, size = CHUNKS[chunk]
    step = 32
    return pl.pallas_call(
        dequant_kernel,
        grid_spec=pltpu.PrefetchScalarGridSpec(
            num_scalar_prefetch=1,
            grid=(size // step,),
            in_specs=[
                pl.BlockSpec((step, width), lambda i, half: (first // step + i, half[0])),
                pl.BlockSpec((step, scales.shape[1]), lambda i, half: (first // step + i, 0)),
            ]
            + [ANYWHERE] * len(earlier),
            out_specs=pl.BlockSpec((step, width), lambda i, half: (i, 0)),
        ),
        out_shape=jax.ShapeDtypeStruct((size, width), jnp.bfloat16),
        cost_estimate=pl.CostEstimate(
            flops=2 * size * width, bytes_accessed=6 * size * width, transcendentals=0
        ),
    )(half_id, codes, scales, *earlier)


def level_kernel(high_ref, own_ref, partner_ref, *refs):
    out_ref = refs[-1]
    own = own_ref[...].astype(jnp.float32)
    partner = partner_ref[...].astype(jnp.float32)
    out_ref[...] = (jnp.where(high_ref[0] == 0, own, -own) + partner).astype(jnp.bfloat16)


def level_step(value, bit, earlier=()):
    partner = flipped(value, "tp", bit)
    high = (lax.axis_index("tp") & bit).reshape(1)
    size, width = value.shape
    step = size // 4 if size % 64 == 0 else size // 2
    spec = pl.BlockSpec((step, width), lambda i, high: (i, 0))
    return pl.pallas_call(
        level_kernel,
        grid_spec=pltpu.PrefetchScalarGridSpec(
            num_scalar_prefetch=1,
            grid=(size // step,),
            in_specs=[spec, spec] + [ANYWHERE] * len(earlier),
            out_specs=spec,
        ),
        out_shape=jax.ShapeDtypeStruct(value.shape, jnp.bfloat16),
        cost_estimate=pl.CostEstimate(
            flops=2 * size * width, bytes_accessed=6 * size * width, transcendentals=0
        ),
    )(high, value, partner, *earlier)


def project_kernel(chunks, half_ref, rows_ref, attn_ref, out_own, out_near, *refs):
    weights = refs[: 4 * len(chunks)]
    out_ref, total = refs[4 * len(chunks) :]
    step = pl.program_id(0)
    steps = pl.num_programs(0)

    def joined(parts):
        return jnp.concatenate(parts, axis=0)

    @pl.when(step == 0)
    def _():
        side = []
        for first, size in chunks:
            side += [out_own[first : first + size, :], out_near[first : first + size, :]]
        total[...] = lax.dot_general(
            attn_ref[...], joined(side), NT, preferred_element_type=jnp.float32
        )

    @pl.when(step < steps // 2)
    def _():
        part = joined([ref[...] for ref in weights[0::2]])
        total[...] += lax.dot_general(
            rows_ref[...], part, NT, preferred_element_type=jnp.float32
        )

    @pl.when(step >= steps // 2)
    def _():
        part = joined([ref[...] for ref in weights[1::2]])
        total[...] += lax.dot_general(
            rows_ref[...], part, NT, preferred_element_type=jnp.float32
        )

    @pl.when(step == steps - 1)
    def _():
        out_ref[...] = total[...].astype(jnp.bfloat16)


def project(half_id, rows_in, attn, out_own, out_near, weights, chunks):
    rows, width = rows_in.shape
    half = width // 2
    steps = 6
    depth = width // steps
    last = steps // 2 - 1
    columns = 2 * sum(size for _, size in chunks)
    weight_specs = []
    for _, size in chunks:
        weight_specs += [
            pl.BlockSpec((size, depth), lambda i, h: (0, jnp.minimum(i, last))),
            pl.BlockSpec((size, depth), lambda i, h: (0, jnp.maximum(i - last - 1, 0))),
        ] * 2

    def whole(array):
        return pl.BlockSpec(array.shape, lambda i, h: (0, 0))

    return pl.pallas_call(
        lambda *refs: project_kernel(chunks, *refs),
        grid_spec=pltpu.PrefetchScalarGridSpec(
            num_scalar_prefetch=1,
            grid=(steps,),
            in_specs=[
                pl.BlockSpec(
                    (rows, depth), lambda i, h: (0, lax.rem(i + h[0] * (last + 1), steps))
                ),
                whole(attn),
                whole(out_own),
                whole(out_near),
            ]
            + weight_specs,
            out_specs=pl.BlockSpec((rows, columns), lambda i, h: (0, 0)),
            scratch_shapes=[pltpu.VMEM((rows, columns), jnp.float32)],
        ),
        out_shape=jax.ShapeDtypeStruct((rows, columns), jnp.bfloat16),
        compiler_params=pltpu.CompilerParams(vmem_limit_bytes=56 << 20),
        cost_estimate=pl.CostEstimate(
            flops=2 * rows * (width + attn.shape[1]) * columns,
            bytes_accessed=2 * (rows + columns) * (width + attn.shape[1]),
            transcendentals=0,
        ),
    )(half_id, rows_in, attn, out_own, out_near, *weights)


def turned(head, cosine, signed_sine):
    head = head.astype(jnp.float32)
    return (head * cosine + pltpu.roll(head, HD // 2, 1) * signed_sine).astype(jnp.bfloat16)


def keys_kernel(pairs_ref, cosine_ref, sine_ref, out_ref):
    keys = pairs_ref.shape[1] // 2
    for first in range(0, keys, HD):
        out_ref[:, first : first + HD] = turned(
            pairs_ref[:, first : first + HD], cosine_ref[...], sine_ref[...]
        )
    out_ref[:, keys:] = pairs_ref[:, keys:]


def rotate_keys(pairs, cosine, signed_sine):
    rows, width = pairs.shape
    step = rows // 2
    return pl.pallas_call(
        keys_kernel,
        grid=(rows // step,),
        in_specs=[
            pl.BlockSpec((step, width), lambda i: (i, 0)),
            pl.BlockSpec((step, HD), lambda i: (i, 0)),
            pl.BlockSpec((step, HD), lambda i: (i, 0)),
        ],
        out_specs=pl.BlockSpec((step, width), lambda i: (i, 0)),
        out_shape=jax.ShapeDtypeStruct(pairs.shape, jnp.bfloat16),
        cost_estimate=pl.CostEstimate(
            flops=4 * rows * width, bytes_accessed=4 * rows * width, transcendentals=0
        ),
    )(pairs, cosine, signed_sine)


def attend_kernel(
    query_ref, cosine_ref, sine_ref, key0, value0, key1, value1, key2, value2, out_ref
):
    rows = query_ref.shape[0]
    half = rows // 2
    heads = query_ref.shape[1] // HD
    for part in range(2):
        low = part * half
        here = slice(low, low + half)
        own = slice(0, low + half)
        old = slice(low, rows)
        query = jnp.concatenate(
            [
                turned(
                    query_ref[here, head * HD : (head + 1) * HD],
                    cosine_ref[here, :],
                    sine_ref[here, :],
                )
                for head in range(heads)
            ],
            axis=0,
        )

        def score(keys):
            return (
                lax.dot_general(query, keys, NT, preferred_element_type=jnp.float32) * SCORE_SCALE
            )

        def places(count, first):
            query_at = lax.broadcasted_iota(jnp.int32, (heads, half, count), 1) + low
            key_at = lax.broadcasted_iota(jnp.int32, (heads, half, count), 2) + first
            shape = (heads * half, count)
            return query_at.reshape(shape), key_at.reshape(shape)

        score0, score1, score2 = score(key0[own, :]), score(key1[...]), score(key2[old, :])
        query_at, key_at = places(low + half, 0)
        score0 = jnp.where(key_at <= query_at, score0, -jnp.inf)
        query_at, key_at = places(rows - low, low)
        score2 = jnp.where(key_at > query_at, score2, -jnp.inf)
        top = jnp.maximum(
            jnp.max(score0, axis=1, keepdims=True),
            jnp.maximum(
                jnp.max(score1, axis=1, keepdims=True), jnp.max(score2, axis=1, keepdims=True)
            ),
        )
        mass = jnp.zeros_like(top)
        total = jnp.zeros((heads * half, HD), jnp.float32)
        for scores, values in (
            (score0, value0[own, :]),
            (score1, value1[...]),
            (score2, value2[old, :]),
        ):
            weight = jnp.exp(scores - top)
            mass += jnp.sum(weight, axis=1, keepdims=True)
            total += jnp.dot(
                weight.astype(jnp.bfloat16), values, preferred_element_type=jnp.float32
            )
        total = (total / mass).astype(jnp.bfloat16)
        for head in range(heads):
            out_ref[here, head * HD : (head + 1) * HD] = total[head * half : (head + 1) * half]


def attend(queries, cosine, signed_sine, blocks):
    rows, width = queries.shape
    kv_heads = blocks[0].shape[1] // (2 * HD)
    wide = width // kv_heads
    key_spec = pl.BlockSpec((rows, HD), lambda i: (0, i))
    value_spec = pl.BlockSpec((rows, HD), lambda i: (0, kv_heads + i))
    table_spec = pl.BlockSpec((rows, HD), lambda i: (0, 0))
    query_spec = pl.BlockSpec((rows, wide), lambda i: (0, i))
    return pl.pallas_call(
        attend_kernel,
        grid=(kv_heads,),
        in_specs=[query_spec, table_spec, table_spec] + [key_spec, value_spec] * 3,
        out_specs=query_spec,
        out_shape=jax.ShapeDtypeStruct(queries.shape, jnp.bfloat16),
        compiler_params=pltpu.CompilerParams(vmem_limit_bytes=56 << 20),
        cost_estimate=pl.CostEstimate(
            flops=4 * rows * width * 3 * rows,
            bytes_accessed=2 * rows * width * 8,
            transcendentals=3 * rows * rows * width // HD,
        ),
    )(queries, cosine, signed_sine, *[block for block in blocks for _ in range(2)])


def flipped(value, axis, bit):
    return lax.ppermute(value, axis, [(i, i ^ bit) for i in range(lax.axis_size(axis))])


def planned(
    queries, key_value, window_cache, span_start, hidden, down_codes, down_scales, out_weight
):
    half_id = lax.axis_index("group").reshape(1)
    seq_index = lax.axis_index("seq")
    core = seq_index & 1
    side = seq_index >> 1
    tok_rows = queries.shape[0]
    first_pos = span_start[0]

    half_groups = down_scales.shape[0] // 2
    scales = lax.dynamic_slice_in_dim(down_scales, half_id[0] * half_groups, half_groups, 0)
    scales = scales.T.astype(jnp.float32)
    codes = down_codes.T
    out_own = out_weight.T
    piece_a = dequant(half_id, codes, scales, 0)
    piece_b = dequant(half_id, codes, scales, 1)
    rotated = mix_hidden(hidden, piece_b)
    far_rotated = flipped(rotated, "seq", 2)

    positions = first_pos + seq_index * tok_rows + jnp.arange(tok_rows, dtype=jnp.int32)
    inv_freq = ROPE_BASE ** (-(2.0 * jnp.arange(HD // 2, dtype=jnp.float32)) / HD)
    angles = positions.astype(jnp.float32)[:, None] * inv_freq[None, :]
    cosine, sine = jnp.cos(angles), jnp.sin(angles)
    cosine = jnp.concatenate([cosine, cosine], axis=1)
    signed_sine = jnp.concatenate([-sine, sine], axis=1)
    own_pairs = rotate_keys(key_value.reshape(tok_rows, -1), cosine, signed_sine)
    halo1 = shifted(own_pairs, "seq", 1)
    halo2 = shifted(halo1, "seq", 1)
    cache = window_cache.reshape(WINDOW, -1)
    doubled = jnp.concatenate([cache, cache], axis=0)
    first1 = (first_pos + tok_rows) % WINDOW
    first2 = (first_pos + jnp.minimum(seq_index, 1) * tok_rows) % WINDOW
    cached1 = lax.dynamic_slice_in_dim(doubled, first1, tok_rows, 0)
    cached2 = lax.dynamic_slice_in_dim(doubled, first2, tok_rows, 0)
    before1 = jnp.where(seq_index >= 1, halo1, cached1)
    before2 = jnp.where(seq_index >= 2, halo2, cached2)
    attended = attend(queries, cosine, signed_sine, [own_pairs, before1, before2])
    far_attended = flipped(attended, "seq", 2)
    out_near = flipped(out_own, "seq", 1)

    piece_a = level_step(piece_a, 2)
    piece_b = level_step(piece_b, 1, (piece_a,))
    piece_c = dequant(half_id, codes, scales, 2, (piece_a,))
    piece_a = level_step(piece_a, 1)
    piece_b = level_step(piece_b, 2)
    piece_c = level_step(piece_c, 1, (piece_b,))
    piece_c = level_step(piece_c, 2)

    def spread(piece):
        across = flipped(piece, "group", 1)
        return [piece, across, flipped(piece, "seq", 1), flipped(across, "seq", 1)]

    def reduced(rows_in, attn, weights, chunks):
        partial = project(half_id, rows_in, attn, out_own, out_near, weights, chunks)
        return lax.psum_scatter(partial, "tp", scatter_dimension=0, tiled=True)

    weights = [spread(piece) for piece in (piece_a, piece_b, piece_c)]
    own_sums = [
        reduced(rotated, attended, part, CHUNKS[chunk : chunk + 1])
        for chunk, part in enumerate(weights)
    ]
    far_sums = [
        reduced(far_rotated, far_attended, weights[0] + weights[1], CHUNKS[:2]),
        reduced(far_rotated, far_attended, weights[2], CHUNKS[2:]),
    ]

    def by_core(sums):
        sums = jnp.concatenate(sums, axis=1)
        own, near, at = [], [], 0
        for _, size in CHUNKS:
            own.append(sums[:, at : at + size])
            near.append(sums[:, at + size : at + 2 * size])
            at += 2 * size
        own, near = jnp.concatenate(own, axis=1), jnp.concatenate(near, axis=1)
        return [jnp.where(core == 0, own, near), jnp.where(core == 0, near, own)]

    here = by_core(own_sums)
    there = by_core([flipped(part, "seq", 2) for part in far_sums])
    columns = [jnp.where(side == 0, a, b) for a, b in zip(here + there, there + here)]
    return jnp.concatenate(columns, axis=1)


def solution(mesh):
    return jax.shard_map(
        planned if fits(mesh) else per_device,
        mesh=mesh,
        in_specs=(
            P(("group", "seq"), "tp"),
            P(("group", "seq"), None, "tp"),
            P("group", None, "tp"),
            P("group"),
            P(("group", "seq"), "tp"),
            P("tp", "seq"),
            P("tp", "seq"),
            P("tp", "seq"),
        ),
        out_specs=P(("group", "seq", "tp"), None),
        check_vma=False,
    )
```

```python
import jax
import jax.numpy as jnp
import numpy as np
from jax import lax
from jax.experimental import pallas as pl
from jax.experimental.pallas import tpu as pltpu
from jax.sharding import PartitionSpec as P

HD = 128
WINDOW = 1024
GROUP = 128


ROPE_BASE = 10000.0
SCORE_SCALE = 168.0 ** (-0.5)
CODE_STEP = 2.0 ** (-14)
INV_ROOT = 1344.0 ** (-0.5)


def shifted(value, axis, steps):
    count = lax.axis_size(axis)
    first, last = (max(0, -steps), min(count, count - steps))
    return lax.ppermute(value, axis, [(source, source + steps) for source in range(first, last)])


def swapped(x, axis, stride):
    return lax.ppermute(x, axis, [(i, i ^ 1 << stride) for i in range(lax.axis_size(axis))])


def bit_total(value_now):
    return (value_now & 1) + (value_now >> 1 & 1) + (value_now >> 2 & 1)


def build_tables():
    prime_order = 167
    residues = set((value_now * value_now % prime_order for value_now in range(1, prime_order)))
    legendre = [0] + [1 if value_now in residues else -1 for value_now in range(1, prime_order)]
    paley_table = np.eye(prime_order + 1)
    paley_table[0, 1:] += 1.0
    paley_table[1:, 0] -= 1.0
    for row_index in range(prime_order):
        for col_index in range(prime_order):
            paley_table[row_index + 1, col_index + 1] += legendre[
                (col_index - row_index) % prime_order
            ]
    sylvester = np.array(
        [
            [(-1.0) ** bit_total(left_bit & right_bit) for right_bit in range(8)]
            for left_bit in range(8)
        ]
    )
    return (paley_table, sylvester)


def rotary(values, cosine, sine_part):
    half_dim = values.shape[-1] // 2
    first_half = values[..., :half_dim]
    second_half = values[..., half_dim:]
    return jnp.concatenate(
        [
            first_half * cosine - second_half * sine_part,
            second_half * cosine + first_half * sine_part,
        ],
        axis=-1,
    )


def section_pairs(blocks_now, section_level):
    row_count, block_count, width_cols = blocks_now.shape
    paired = blocks_now.reshape(
        row_count, block_count >> section_level + 1, 2, 1 << section_level, width_cols
    ).astype(jnp.float32)
    upper_half = paired[:, :, 0]
    lower_half = paired[:, :, 1]
    mixed = jnp.stack([upper_half + lower_half, upper_half - lower_half], axis=2)
    return mixed.astype(jnp.bfloat16).reshape(row_count, block_count, width_cols)


def per_device(
    queries, key_value, window_cache, span_start, hidden, down_codes, down_scales, out_weight
):
    tok_rows = queries.shape[0]
    tp_count = lax.axis_size("tp")
    seq_index = lax.axis_index("seq")
    tp_index = lax.axis_index("tp")
    heads_dev = queries.shape[1] // HD
    kv_dev = key_value.shape[2] // HD
    group_size = heads_dev // kv_dev
    first_pos = span_start[0]
    positions = first_pos + seq_index * tok_rows + jnp.arange(tok_rows, dtype=jnp.int32)
    inv_freq = ROPE_BASE ** (-(2.0 * jnp.arange(HD // 2, dtype=jnp.float32)) / HD)
    angles = positions.astype(jnp.float32)[:, None] * inv_freq[None, :]
    cosine = jnp.cos(angles)[:, None, :]
    sine_part = jnp.sin(angles)[:, None, :]
    query_rot = rotary(
        queries.reshape(tok_rows, heads_dev, HD).astype(jnp.float32), cosine, sine_part
    ).astype(jnp.bfloat16)
    key_rot = rotary(
        key_value[:, 0].reshape(tok_rows, kv_dev, HD).astype(jnp.float32), cosine, sine_part
    ).astype(jnp.bfloat16)
    own_pairs = jnp.stack([key_rot.reshape(tok_rows, kv_dev * HD), key_value[:, 1]], axis=1)
    reach_blocks = WINDOW // tok_rows
    earlier = []
    moving = own_pairs
    for hop_count in range(reach_blocks):
        moving = shifted(moving, "seq", 1)
        earlier.insert(0, moving)
    halo_rows = jnp.concatenate(earlier, axis=0)
    doubled = jnp.concatenate([window_cache, window_cache], axis=0)
    ordered = lax.dynamic_slice_in_dim(doubled, first_pos % WINDOW, WINDOW, 0)
    padded_cache = jnp.concatenate([ordered, jnp.zeros_like(ordered)], axis=0)
    from_cache = lax.dynamic_slice_in_dim(
        padded_cache, jnp.minimum(seq_index * tok_rows, WINDOW), WINDOW, 0
    )
    halo_rows = halo_rows + from_cache
    all_rows = jnp.concatenate([halo_rows, own_pairs], axis=0)
    key_count = all_rows.shape[0]
    key_rows = all_rows[:, 0].reshape(key_count, kv_dev, HD)
    value_rows = all_rows[:, 1].reshape(key_count, kv_dev, HD)
    grouped = query_rot.reshape(tok_rows, kv_dev, group_size, HD)
    scores = (
        jnp.einsum("qkgd,skd->kgqs", grouped, key_rows, preferred_element_type=jnp.float32)
        * SCORE_SCALE
    )
    query_ids = jnp.arange(tok_rows)[:, None]
    key_ids = jnp.arange(key_count)[None, :]
    allowed = (key_ids > query_ids) & (key_ids <= query_ids + WINDOW)
    scores = jnp.where(allowed, scores, -jnp.inf)
    top_score = jnp.max(scores, axis=-1, keepdims=True)
    weights_soft = jnp.exp(scores - top_score)
    weights_soft = (weights_soft / jnp.sum(weights_soft, axis=-1, keepdims=True)).astype(
        jnp.bfloat16
    )
    attended = jnp.einsum(
        "kgqs,skd->qkgd", weights_soft, value_rows, preferred_element_type=jnp.float32
    )
    attended = attended.astype(jnp.bfloat16).reshape(tok_rows, heads_dev * HD)
    paley_np, sylvester_np = build_tables()
    paley_table = jnp.asarray(paley_np, dtype=jnp.bfloat16)
    sylvester = jnp.asarray(sylvester_np, dtype=jnp.float32)
    local_blocks = hidden.shape[1] // 1344
    local_levels = local_blocks.bit_length() - 1
    parts_now = hidden.reshape(tok_rows, local_blocks, 8, 168)
    mixed = jnp.einsum("nbac,cd->nbad", parts_now, paley_table, preferred_element_type=jnp.float32)
    mixed = (
        jnp.einsum("nbad,ae->nbed", mixed, sylvester, precision=lax.Precision.HIGHEST) * INV_ROOT
    )
    blocks_now = mixed.reshape(tok_rows, local_blocks, 1344).astype(jnp.bfloat16)
    for section_level in range(local_levels):
        blocks_now = section_pairs(blocks_now, section_level)
    for bit_index in range(tp_count.bit_length() - 1):
        partner = swapped(blocks_now, "tp", bit_index)
        high_side = jnp.right_shift(tp_index, bit_index) % 2
        own_values = blocks_now.astype(jnp.float32)
        other_values = partner.astype(jnp.float32)
        blocks_now = jnp.where(
            high_side == 0, own_values + other_values, other_values - own_values
        ).astype(jnp.bfloat16)
    rotated = blocks_now.reshape(tok_rows, local_blocks * 1344)
    joined = jnp.concatenate([rotated, attended], axis=1)
    group_count = down_scales.shape[0]
    col_count = down_codes.shape[1]
    down_weight = (
        (down_codes.reshape(group_count, GROUP, col_count) - 8) * down_scales[:, None, :]
    ).astype(jnp.float32) * CODE_STEP
    down_rows = down_weight.astype(jnp.bfloat16).reshape(group_count * GROUP, col_count)
    stacked = jnp.concatenate([down_rows, out_weight], axis=0)
    partials = jnp.dot(
        joined,
        lax.all_gather(stacked, "seq", axis=1, tiled=True),
        preferred_element_type=jnp.float32,
    )
    layer_update = lax.psum_scatter(
        partials.astype(jnp.bfloat16), "tp", scatter_dimension=0, tiled=True
    )
    return layer_update


BLOCK = 1344
PADDED = 1408
CHUNKS = ((0, 192), (192, 192), (384, 144), (528, 144))
NT = (((1,), (1,)), ((), ()))
ANYWHERE = pl.BlockSpec(memory_space=pl.ANY)


def cost(microseconds):
    return pl.CostEstimate(
        flops=1 + int(microseconds * 1.15e9), bytes_accessed=1, transcendentals=0
    )


def fits(mesh):
    return dict(mesh.shape) == {"group": 2, "seq": 4, "tp": 4}


def mix_tables():
    paley_np, sylvester_np = build_tables()
    mix_np = np.kron(sylvester_np, paley_np)
    low = np.zeros((PADDED, PADDED), np.float32)
    high = np.zeros((PADDED, PADDED), np.float32)
    low[:BLOCK, :BLOCK] = mix_np
    high[PADDED - BLOCK :, :BLOCK] = mix_np
    return jnp.asarray(np.stack([low, high]), dtype=jnp.bfloat16)


def mix_kernel(hidden_ref, table_ref, *refs):
    out_ref = refs[-1]
    gap = PADDED - BLOCK
    pair = 2 * BLOCK

    def product(first, table):
        return jnp.dot(
            hidden_ref[:, first : first + PADDED],
            table_ref[table],
            preferred_element_type=jnp.float32,
        )

    sums, differences = [], []
    for half in range(2):
        even = product(half * pair, 0)
        odd = product(half * pair + BLOCK - gap, 1)
        sums.append(even + odd)
        differences.append(even - odd)
    for half in range(2):
        if half == 0:
            even, odd = sums[0] + sums[1], differences[0] + differences[1]
        else:
            even, odd = sums[0] - sums[1], differences[0] - differences[1]
        even, odd = even * INV_ROOT, pltpu.roll(odd * INV_ROOT, gap, 1)
        first, edge = half * pair, BLOCK - gap
        out_ref[:, first : first + edge] = even[:, :edge].astype(jnp.bfloat16)
        out_ref[:, first + edge : first + PADDED] = (even[:, edge:] + odd[:, : 2 * gap]).astype(
            jnp.bfloat16
        )
        out_ref[:, first + PADDED : first + pair] = odd[:, 2 * gap :].astype(jnp.bfloat16)


def mix_hidden(hidden, *earlier):
    rows, width = hidden.shape
    step = 256
    return pl.pallas_call(
        mix_kernel,
        grid=(rows // step,),
        in_specs=[
            pl.BlockSpec((step, width), lambda i: (i, 0)),
            pl.BlockSpec((2, PADDED, PADDED), lambda i: (0, 0, 0)),
        ]
        + [ANYWHERE] * len(earlier),
        out_specs=pl.BlockSpec((step, width), lambda i: (i, 0)),
        out_shape=jax.ShapeDtypeStruct((rows, width), jnp.bfloat16),
        compiler_params=pltpu.CompilerParams(vmem_limit_bytes=56 << 20),
        cost_estimate=cost(16),
    )(hidden, mix_tables(), *earlier)


def dequant_kernel(first, half_ref, codes_ref, scales_ref, spread_ref, *refs):
    out_ref, wide = refs[-2:]
    step = codes_ref.shape[0]

    @pl.when(pl.program_id(0) == 0)
    def _():
        scales = scales_ref[:, first : first + wide.shape[0]].astype(jnp.bfloat16)
        wide[...] = lax.dot_general(
            scales, spread_ref[...], (((0,), (0,)), ((), ())), preferred_element_type=jnp.float32
        )

    rows = pl.ds(pl.multiple_of(pl.program_id(0) * step, step), step)
    out_ref[...] = ((codes_ref[...] - 8).astype(jnp.float32) * wide[rows, :]).astype(jnp.bfloat16)


def dequant(half_id, codes, scales, chunk, earlier=()):
    width = codes.shape[1] // 2
    first, size = CHUNKS[chunk]
    step = 48
    groups = scales.shape[0]
    spread = np.repeat(np.eye(groups, dtype=np.float32) * CODE_STEP, GROUP, axis=1)
    return pl.pallas_call(
        lambda *refs: dequant_kernel(first, *refs),
        grid_spec=pltpu.PrefetchScalarGridSpec(
            num_scalar_prefetch=1,
            grid=(size // step,),
            in_specs=[
                pl.BlockSpec((step, width), lambda i, half: (first // step + i, half[0])),
                pl.BlockSpec(scales.shape, lambda i, half: (0, 0)),
                pl.BlockSpec((groups, width), lambda i, half: (0, half[0])),
            ]
            + [ANYWHERE] * len(earlier),
            out_specs=pl.BlockSpec((step, width), lambda i, half: (i, 0)),
            scratch_shapes=[pltpu.VMEM((size, width), jnp.float32)],
        ),
        out_shape=jax.ShapeDtypeStruct((size, width), jnp.bfloat16),
        cost_estimate=cost(3),
    )(half_id, codes, scales, jnp.asarray(spread, dtype=jnp.bfloat16), *earlier)


def level_kernel(sign_ref, own_ref, partner_ref, *refs):
    out_ref = refs[-1]
    sign = sign_ref[0].astype(jnp.float32).astype(jnp.bfloat16)
    out_ref[...] = own_ref[...] * sign + partner_ref[...]


def level_step(value, bit, earlier=()):
    partner = flipped(value, "tp", bit)
    sign = jnp.where(lax.axis_index("tp") & bit == 0, 1, -1).reshape(1)
    size, width = value.shape
    step = 96 if size % 96 == 0 else 48
    spec = pl.BlockSpec((step, width), lambda i, sign: (i, 0))
    return pl.pallas_call(
        level_kernel,
        grid_spec=pltpu.PrefetchScalarGridSpec(
            num_scalar_prefetch=1,
            grid=(size // step,),
            in_specs=[spec, spec] + [ANYWHERE] * len(earlier),
            out_specs=spec,
        ),
        out_shape=jax.ShapeDtypeStruct(value.shape, jnp.bfloat16),
        cost_estimate=cost(3),
    )(sign, value, partner, *earlier)


def gate_kernel(*refs):
    pass


def gate(value, *earlier):
    return pl.pallas_call(
        gate_kernel,
        in_specs=[ANYWHERE] * (1 + len(earlier)),
        out_specs=ANYWHERE,
        out_shape=jax.ShapeDtypeStruct(value.shape, value.dtype),
        input_output_aliases={0: 0},
        cost_estimate=cost(0),
    )(value, *earlier)


def project_kernel(chunks, count, place_ref, *refs):
    row_refs, attn_refs, out_side = refs[:count], refs[count : 2 * count], refs[2 * count]
    weights = refs[2 * count + 1 : 2 * count + 1 + 2 * len(chunks)]
    out_ref, total = refs[-2:]
    step = pl.program_id(0)
    steps = pl.num_programs(0)
    rows = row_refs[0].shape[0]
    shards = out_ref.shape[0]
    kept = rows // shards

    def add(parts, sources, first):
        part = jnp.concatenate(parts, axis=0)
        for place, ref in enumerate(sources):
            lanes = slice(place * rows, (place + 1) * rows)
            value = lax.dot_general(part, ref[...], NT, preferred_element_type=jnp.float32)
            total[:, lanes] = value if first else total[:, lanes] + value

    @pl.when(step == 0)
    def _():
        add([out_side[first : first + size, :] for first, size in chunks], attn_refs, True)

    @pl.when(step < steps // 2)
    def _():
        add([ref[...] for ref in weights[0::2]], row_refs, False)

    @pl.when(step >= steps // 2)
    def _():
        add([ref[...] for ref in weights[1::2]], row_refs, False)

    @pl.when(step == steps - 1)
    def _():
        for shard in range(shards):
            for place in range(count):
                first = place * rows + shard * kept
                out_ref[shard, :, place * kept : (place + 1) * kept] = total[
                    :, first : first + kept
                ].astype(jnp.bfloat16)


def project(place, shards, row_parts, attn, flips, out_side, weights, chunks, earlier=()):
    count = len(row_parts)
    rows, width = row_parts[0].shape
    steps = 6
    depth = width // steps
    last = steps // 2 - 1
    columns = sum(size for _, size in chunks)
    weight_specs = []
    for _, size in chunks:
        weight_specs += [
            pl.BlockSpec((size, depth), lambda i, h: (0, jnp.minimum(i, last))),
            pl.BlockSpec((size, depth), lambda i, h: (0, jnp.maximum(i - last - 1, 0))),
        ]
    row_spec = pl.BlockSpec((rows, depth), lambda i, h: (0, lax.rem(i + h[0] * (last + 1), steps)))

    def attn_spec(flip):
        return pl.BlockSpec((rows, attn.shape[1]), lambda i, h: (h[1] ^ flip, 0))

    shape = (shards, columns, count * rows // shards)
    return pl.pallas_call(
        lambda *refs: project_kernel(chunks, count, *refs),
        grid_spec=pltpu.PrefetchScalarGridSpec(
            num_scalar_prefetch=1,
            grid=(steps,),
            in_specs=[row_spec] * count
            + [attn_spec(flip) for flip in flips]
            + [pl.BlockSpec(out_side.shape, lambda i, h: (0, 0))]
            + weight_specs
            + [ANYWHERE] * len(earlier),
            out_specs=pl.BlockSpec(shape, lambda i, h: (0, 0, 0)),
            scratch_shapes=[pltpu.VMEM((columns, count * rows), jnp.float32)],
        ),
        out_shape=jax.ShapeDtypeStruct(shape, jnp.bfloat16),
        compiler_params=pltpu.CompilerParams(vmem_limit_bytes=56 << 20),
        cost_estimate=cost(10),
    )(place, *row_parts, *[attn] * count, out_side, *weights, *earlier)


def turned(head, cosine, signed_sine):
    head = head.astype(jnp.float32)
    return (head * cosine + pltpu.roll(head, HD // 2, 1) * signed_sine).astype(jnp.bfloat16)


def attend_kernel(
    place_ref,
    query_ref,
    cosine_ref,
    sine_ref,
    key0,
    value0,
    key1,
    value1,
    cached_key1,
    cached_value1,
    key2,
    value2,
    cached_key2,
    cached_value2,
    out_ref,
):
    rows = query_ref.shape[0]

    def chosen(block, halo, cached):
        return jnp.where(place_ref[0] >= block, halo[...], cached[...])

    key1, value1 = chosen(1, key1, cached_key1), chosen(1, value1, cached_value1)
    key2, value2 = chosen(2, key2, cached_key2), chosen(2, value2, cached_value2)
    keys = [
        turned(
            key,
            cosine_ref[block * rows : (block + 1) * rows, :],
            sine_ref[block * rows : (block + 1) * rows, :],
        )
        for block, key in enumerate((key0[...], key1, key2))
    ]
    half = rows // 2
    heads = query_ref.shape[1] // HD
    for part in range(2):
        low = part * half
        here = slice(low, low + half)
        own = slice(0, low + half)
        old = slice(low, rows)
        query = jnp.concatenate(
            [
                turned(
                    query_ref[here, head * HD : (head + 1) * HD],
                    cosine_ref[here, :],
                    sine_ref[here, :],
                )
                for head in range(heads)
            ],
            axis=0,
        )

        def score(block):
            return (
                lax.dot_general(query, block, NT, preferred_element_type=jnp.float32) * SCORE_SCALE
            )

        def places(count, first):
            query_at = lax.broadcasted_iota(jnp.int32, (heads, half, count), 1) + low
            key_at = lax.broadcasted_iota(jnp.int32, (heads, half, count), 2) + first
            shape = (heads * half, count)
            return query_at.reshape(shape), key_at.reshape(shape)

        score0, score1, score2 = score(keys[0][own, :]), score(keys[1]), score(keys[2][old, :])
        query_at, key_at = places(low + half, 0)
        score0 = jnp.where(key_at <= query_at, score0, -jnp.inf)
        query_at, key_at = places(rows - low, low)
        score2 = jnp.where(key_at > query_at, score2, -jnp.inf)
        top = jnp.maximum(
            jnp.max(score0, axis=1, keepdims=True),
            jnp.maximum(
                jnp.max(score1, axis=1, keepdims=True), jnp.max(score2, axis=1, keepdims=True)
            ),
        )
        mass = jnp.zeros_like(top)
        total = jnp.zeros((heads * half, HD), jnp.float32)
        for scores, values in (
            (score0, value0[own, :]),
            (score1, value1),
            (score2, value2[old, :]),
        ):
            weight = jnp.exp(scores - top)
            mass += jnp.sum(weight, axis=1, keepdims=True)
            total += jnp.dot(
                weight.astype(jnp.bfloat16), values, preferred_element_type=jnp.float32
            )
        total = (total / mass).astype(jnp.bfloat16)
        for head in range(heads):
            out_ref[here, head * HD : (head + 1) * HD] = total[head * half : (head + 1) * half]


def attend(place, queries, cosine, signed_sine, pairs, all_pairs, cached1, cached2):
    rows, width = queries.shape
    kv_heads = pairs.shape[1] // (2 * HD)
    wide = width // kv_heads

    def specs(back):
        def row(p):
            return 0 if back is None else jnp.maximum(p[0] - back, 0)

        return [
            pl.BlockSpec((rows, HD), lambda i, p: (row(p), i)),
            pl.BlockSpec((rows, HD), lambda i, p: (row(p), kv_heads + i)),
        ]

    table_spec = pl.BlockSpec(cosine.shape, lambda i, p: (0, 0))
    query_spec = pl.BlockSpec((rows, wide), lambda i, p: (0, i))
    return pl.pallas_call(
        attend_kernel,
        grid_spec=pltpu.PrefetchScalarGridSpec(
            num_scalar_prefetch=1,
            grid=(kv_heads,),
            in_specs=[query_spec, table_spec, table_spec]
            + specs(None)
            + specs(1)
            + specs(None)
            + specs(2)
            + specs(None),
            out_specs=query_spec,
        ),
        out_shape=jax.ShapeDtypeStruct(queries.shape, jnp.bfloat16),
        compiler_params=pltpu.CompilerParams(vmem_limit_bytes=56 << 20),
        cost_estimate=cost(13),
    )(
        place,
        queries,
        cosine,
        signed_sine,
        pairs,
        pairs,
        all_pairs,
        all_pairs,
        cached1,
        cached1,
        all_pairs,
        all_pairs,
        cached2,
        cached2,
    )


def flipped(value, axis, bit):
    return lax.ppermute(value, axis, [(i, i ^ bit) for i in range(lax.axis_size(axis))])


def planned(
    queries, key_value, window_cache, span_start, hidden, down_codes, down_scales, out_weight
):
    half_id = lax.axis_index("group").reshape(1)
    seq_index = lax.axis_index("seq")
    core = seq_index & 1
    side = seq_index >> 1
    tok_rows = queries.shape[0]

    pairs = key_value.reshape(tok_rows, -1)
    all_pairs = lax.all_gather(pairs, "seq", axis=0, tiled=True)

    codes = down_codes.T
    out_own = out_weight.T
    piece_a = dequant(half_id, codes, down_scales, 0)
    piece_c = dequant(half_id, codes, down_scales, 1, (piece_a, pairs))
    rotated = mix_hidden(hidden, piece_c)
    piece_b = dequant(half_id, codes, down_scales, 2, (rotated,))
    piece_d = dequant(half_id, codes, down_scales, 3, (piece_b,))

    def both_cores(value):
        return [value, flipped(value, "seq", 1)]

    own_rows = both_cores(rotated)
    piece_a = level_step(piece_a, 2)
    piece_c = level_step(piece_c, 1, (piece_a,))
    first_pos = gate(span_start, piece_c)[0]

    block_first = first_pos + (seq_index - jnp.arange(3, dtype=jnp.int32)) * tok_rows
    positions = block_first[:, None] + jnp.arange(tok_rows, dtype=jnp.int32)[None, :]
    inv_freq = ROPE_BASE ** (-(2.0 * jnp.arange(HD // 2, dtype=jnp.float32)) / HD)
    angles = positions.astype(jnp.float32)[:, :, None] * inv_freq
    turn = (seq_index >= jnp.arange(3))[:, None, None]
    cosine, sine = jnp.where(turn, jnp.cos(angles), 1.0), jnp.where(turn, jnp.sin(angles), 0.0)
    cosine = jnp.concatenate([cosine, cosine], axis=2).reshape(-1, HD)
    signed_sine = jnp.concatenate([-sine, sine], axis=2).reshape(-1, HD)
    cache = gate(window_cache, piece_c).reshape(WINDOW, -1)
    doubled = jnp.concatenate([cache, cache], axis=0)
    first1 = (first_pos + tok_rows) % WINDOW
    first2 = (first_pos + jnp.minimum(seq_index, 1) * tok_rows) % WINDOW
    cached1 = lax.dynamic_slice_in_dim(doubled, first1, tok_rows, 0)
    cached2 = lax.dynamic_slice_in_dim(doubled, first2, tok_rows, 0)
    attended = attend(
        seq_index.reshape(1), queries, cosine, signed_sine, pairs, all_pairs, cached1, cached2
    )

    piece_b = level_step(piece_b, 2, (piece_c, attended))
    piece_d = level_step(piece_d, 1, (piece_b, own_rows[1]))
    piece_a = level_step(piece_a, 1, (piece_d,))
    across_a = flipped(piece_a, "group", 1)
    piece_c = level_step(piece_c, 2, (piece_a,))
    across_c = flipped(piece_c, "group", 1)
    piece_b = level_step(piece_b, 1, (piece_c, across_a))
    across_b = flipped(piece_b, "group", 1)
    piece_d = level_step(piece_d, 2, (piece_b, across_c))
    across_d = flipped(piece_d, "group", 1)

    shards = lax.axis_size("tp")
    place = jnp.stack([half_id[0], seq_index])
    all_attended = lax.all_gather(attended, "seq", axis=0, tiled=True)

    def reduced(rows, flips, weights, chunks, earlier=()):
        partial = project(
            place, shards, rows, all_attended, flips, out_own, weights, chunks, earlier
        )
        return lax.psum_scatter(partial, "tp", scatter_dimension=0, tiled=True)[0], partial

    early, late = [piece_a, across_a, piece_c, across_c], [piece_b, across_b, piece_d, across_d]
    own_early, own_done = reduced(own_rows, (0, 1), early, CHUNKS[:2], (piece_d,))
    far_rows = both_cores(gate(flipped(rotated, "seq", 2), own_done, across_b))
    far_early, far_done = reduced(far_rows, (2, 3), early, CHUNKS[:2], (across_d,))
    all_late, _ = reduced(own_rows + far_rows, (0, 1, 2, 3), late, CHUNKS[2:], (far_done,))
    kept = tok_rows // shards
    sums = jnp.concatenate([own_early, far_early], axis=1)
    sums = jnp.concatenate([sums, all_late], axis=0)
    strips = [sums[:, i * kept : (i + 1) * kept] for i in range(4)]
    strips = strips[:1] + [flipped(strips[i], "seq", i) for i in (1, 2, 3)]
    strips = [jnp.where(core == 0, strips[i], strips[i ^ 1]) for i in range(4)]
    strips = [jnp.where(side == 0, strips[i], strips[i ^ 2]) for i in range(4)]
    return jnp.concatenate(strips, axis=0).T


def solution(mesh):
    return jax.shard_map(
        planned if fits(mesh) else per_device,
        mesh=mesh,
        in_specs=(
            P(("group", "seq"), "tp"),
            P(("group", "seq"), None, "tp"),
            P("group", None, "tp"),
            P("group"),
            P(("group", "seq"), "tp"),
            P("tp", "seq"),
            P("tp", "seq"),
            P("tp", "seq"),
        ),
        out_specs=P(("group", "seq", "tp"), None),
        check_vma=False,
    )
```

```python
import jax
import jax.numpy as jnp
import numpy as np
from jax import lax
from jax.experimental import pallas as pl
from jax.experimental.pallas import tpu as pltpu
from jax.sharding import PartitionSpec as P

HD = 128
WINDOW = 1024
GROUP = 128


ROPE_BASE = 10000.0
SCORE_SCALE = 168.0 ** (-0.5)
CODE_STEP = 2.0 ** (-14)
INV_ROOT = 1344.0 ** (-0.5)


def shifted(value, axis, steps):
    count = lax.axis_size(axis)
    first, last = (max(0, -steps), min(count, count - steps))
    return lax.ppermute(value, axis, [(source, source + steps) for source in range(first, last)])


def swapped(x, axis, stride):
    return lax.ppermute(x, axis, [(i, i ^ 1 << stride) for i in range(lax.axis_size(axis))])


def bit_total(value_now):
    return (value_now & 1) + (value_now >> 1 & 1) + (value_now >> 2 & 1)


def build_tables():
    prime_order = 167
    residues = set((value_now * value_now % prime_order for value_now in range(1, prime_order)))
    legendre = [0] + [1 if value_now in residues else -1 for value_now in range(1, prime_order)]
    paley_table = np.eye(prime_order + 1)
    paley_table[0, 1:] += 1.0
    paley_table[1:, 0] -= 1.0
    for row_index in range(prime_order):
        for col_index in range(prime_order):
            paley_table[row_index + 1, col_index + 1] += legendre[
                (col_index - row_index) % prime_order
            ]
    sylvester = np.array(
        [
            [(-1.0) ** bit_total(left_bit & right_bit) for right_bit in range(8)]
            for left_bit in range(8)
        ]
    )
    return (paley_table, sylvester)


def rotary(values, cosine, sine_part):
    half_dim = values.shape[-1] // 2
    first_half = values[..., :half_dim]
    second_half = values[..., half_dim:]
    return jnp.concatenate(
        [
            first_half * cosine - second_half * sine_part,
            second_half * cosine + first_half * sine_part,
        ],
        axis=-1,
    )


def section_pairs(blocks_now, section_level):
    row_count, block_count, width_cols = blocks_now.shape
    paired = blocks_now.reshape(
        row_count, block_count >> section_level + 1, 2, 1 << section_level, width_cols
    ).astype(jnp.float32)
    upper_half = paired[:, :, 0]
    lower_half = paired[:, :, 1]
    mixed = jnp.stack([upper_half + lower_half, upper_half - lower_half], axis=2)
    return mixed.astype(jnp.bfloat16).reshape(row_count, block_count, width_cols)


def per_device(
    queries, key_value, window_cache, span_start, hidden, down_codes, down_scales, out_weight
):
    tok_rows = queries.shape[0]
    tp_count = lax.axis_size("tp")
    seq_index = lax.axis_index("seq")
    tp_index = lax.axis_index("tp")
    heads_dev = queries.shape[1] // HD
    kv_dev = key_value.shape[2] // HD
    group_size = heads_dev // kv_dev
    first_pos = span_start[0]
    positions = first_pos + seq_index * tok_rows + jnp.arange(tok_rows, dtype=jnp.int32)
    inv_freq = ROPE_BASE ** (-(2.0 * jnp.arange(HD // 2, dtype=jnp.float32)) / HD)
    angles = positions.astype(jnp.float32)[:, None] * inv_freq[None, :]
    cosine = jnp.cos(angles)[:, None, :]
    sine_part = jnp.sin(angles)[:, None, :]
    query_rot = rotary(
        queries.reshape(tok_rows, heads_dev, HD).astype(jnp.float32), cosine, sine_part
    ).astype(jnp.bfloat16)
    key_rot = rotary(
        key_value[:, 0].reshape(tok_rows, kv_dev, HD).astype(jnp.float32), cosine, sine_part
    ).astype(jnp.bfloat16)
    own_pairs = jnp.stack([key_rot.reshape(tok_rows, kv_dev * HD), key_value[:, 1]], axis=1)
    reach_blocks = WINDOW // tok_rows
    earlier = []
    moving = own_pairs
    for hop_count in range(reach_blocks):
        moving = shifted(moving, "seq", 1)
        earlier.insert(0, moving)
    halo_rows = jnp.concatenate(earlier, axis=0)
    doubled = jnp.concatenate([window_cache, window_cache], axis=0)
    ordered = lax.dynamic_slice_in_dim(doubled, first_pos % WINDOW, WINDOW, 0)
    padded_cache = jnp.concatenate([ordered, jnp.zeros_like(ordered)], axis=0)
    from_cache = lax.dynamic_slice_in_dim(
        padded_cache, jnp.minimum(seq_index * tok_rows, WINDOW), WINDOW, 0
    )
    halo_rows = halo_rows + from_cache
    all_rows = jnp.concatenate([halo_rows, own_pairs], axis=0)
    key_count = all_rows.shape[0]
    key_rows = all_rows[:, 0].reshape(key_count, kv_dev, HD)
    value_rows = all_rows[:, 1].reshape(key_count, kv_dev, HD)
    grouped = query_rot.reshape(tok_rows, kv_dev, group_size, HD)
    scores = (
        jnp.einsum("qkgd,skd->kgqs", grouped, key_rows, preferred_element_type=jnp.float32)
        * SCORE_SCALE
    )
    query_ids = jnp.arange(tok_rows)[:, None]
    key_ids = jnp.arange(key_count)[None, :]
    allowed = (key_ids > query_ids) & (key_ids <= query_ids + WINDOW)
    scores = jnp.where(allowed, scores, -jnp.inf)
    top_score = jnp.max(scores, axis=-1, keepdims=True)
    weights_soft = jnp.exp(scores - top_score)
    weights_soft = (weights_soft / jnp.sum(weights_soft, axis=-1, keepdims=True)).astype(
        jnp.bfloat16
    )
    attended = jnp.einsum(
        "kgqs,skd->qkgd", weights_soft, value_rows, preferred_element_type=jnp.float32
    )
    attended = attended.astype(jnp.bfloat16).reshape(tok_rows, heads_dev * HD)
    paley_np, sylvester_np = build_tables()
    paley_table = jnp.asarray(paley_np, dtype=jnp.bfloat16)
    sylvester = jnp.asarray(sylvester_np, dtype=jnp.float32)
    local_blocks = hidden.shape[1] // 1344
    local_levels = local_blocks.bit_length() - 1
    parts_now = hidden.reshape(tok_rows, local_blocks, 8, 168)
    mixed = jnp.einsum("nbac,cd->nbad", parts_now, paley_table, preferred_element_type=jnp.float32)
    mixed = (
        jnp.einsum("nbad,ae->nbed", mixed, sylvester, precision=lax.Precision.HIGHEST) * INV_ROOT
    )
    blocks_now = mixed.reshape(tok_rows, local_blocks, 1344).astype(jnp.bfloat16)
    for section_level in range(local_levels):
        blocks_now = section_pairs(blocks_now, section_level)
    for bit_index in range(tp_count.bit_length() - 1):
        partner = swapped(blocks_now, "tp", bit_index)
        high_side = jnp.right_shift(tp_index, bit_index) % 2
        own_values = blocks_now.astype(jnp.float32)
        other_values = partner.astype(jnp.float32)
        blocks_now = jnp.where(
            high_side == 0, own_values + other_values, other_values - own_values
        ).astype(jnp.bfloat16)
    rotated = blocks_now.reshape(tok_rows, local_blocks * 1344)
    joined = jnp.concatenate([rotated, attended], axis=1)
    group_count = down_scales.shape[0]
    col_count = down_codes.shape[1]
    down_weight = (
        (down_codes.reshape(group_count, GROUP, col_count) - 8) * down_scales[:, None, :]
    ).astype(jnp.float32) * CODE_STEP
    down_rows = down_weight.astype(jnp.bfloat16).reshape(group_count * GROUP, col_count)
    stacked = jnp.concatenate([down_rows, out_weight], axis=0)
    partials = jnp.dot(
        joined,
        lax.all_gather(stacked, "seq", axis=1, tiled=True),
        preferred_element_type=jnp.float32,
    )
    layer_update = lax.psum_scatter(
        partials.astype(jnp.bfloat16), "tp", scatter_dimension=0, tiled=True
    )
    return layer_update


PIECE = 672
SHIFT = 96
WINDOWED = PIECE + SHIFT
HALF = 336
WIDE = 192
EARLY = ((0, WIDE), (HALF, WIDE))
LATE = ((WIDE, HALF - WIDE), (HALF + WIDE, HALF - WIDE))
NT = (((1,), (1,)), ((), ()))
ANYWHERE = pl.BlockSpec(memory_space=pl.ANY)


def cost(microseconds):
    return pl.CostEstimate(
        flops=1 + int(microseconds * 1.15e9), bytes_accessed=1, transcendentals=0
    )


def fits(mesh):
    return dict(mesh.shape) == {"group": 2, "seq": 4, "tp": 4}


def mix_tables():
    paley_np, sylvester_np = build_tables()
    table = np.zeros((WINDOWED + SHIFT, WINDOWED), np.float32)
    table[SHIFT : SHIFT + PIECE, :PIECE] = np.kron(sylvester_np[:4, :4], paley_np)
    return jnp.asarray(table, dtype=jnp.bfloat16)


def mix_kernel(hidden_ref, table_ref, *refs):
    out_ref = refs[-1]
    rows = hidden_ref.shape[0]
    pair = 4 * PIECE
    pieces = []
    for place in range(4):
        shift = place * PIECE % 128
        first = place * PIECE - shift
        stacked = jnp.concatenate(
            [
                hidden_ref[:, start + first : start + first + WINDOWED] for start in (0, pair)
            ],
            axis=0,
        )
        table = table_ref[SHIFT - shift : SHIFT - shift + WINDOWED, :]
        pieces.append(jnp.dot(stacked, table, preferred_element_type=jnp.float32) * INV_ROOT)
    for bit in (1, 2):
        pieces = [
            pieces[i] + pieces[i ^ bit] if i & bit == 0 else pieces[i ^ bit] - pieces[i]
            for i in range(4)
        ]
    for half in range(2):
        carried = None
        for place in range(4):
            upper, lower = pieces[place][:rows], pieces[place][rows:]
            value = upper + lower if half == 0 else upper - lower
            shift = place * PIECE % 128
            first = half * pair + place * PIECE - shift
            if shift:
                value = pltpu.roll(value, shift, 1)
                value = jnp.concatenate([value[:, :128] + carried, value[:, 128:]], axis=1)
            keep = WINDOWED if place == 3 else WINDOWED - 128
            out_ref[:, first : first + keep] = value[:, :keep].astype(jnp.bfloat16)
            carried = value[:, keep:]


def mix_hidden(hidden, *earlier):
    rows, width = hidden.shape
    step = 256
    return pl.pallas_call(
        mix_kernel,
        grid=(rows // step,),
        in_specs=[
            pl.BlockSpec((step, width), lambda i: (i, 0)),
            pl.BlockSpec((WINDOWED + SHIFT, WINDOWED), lambda i: (0, 0)),
        ]
        + [ANYWHERE] * len(earlier),
        out_specs=pl.BlockSpec((step, width), lambda i: (i, 0)),
        out_shape=jax.ShapeDtypeStruct((rows, width), jnp.bfloat16),
        compiler_params=pltpu.CompilerParams(vmem_limit_bytes=56 << 20),
        cost_estimate=cost(16),
        name="mix",
    )(hidden, mix_tables(), *earlier)


def dequant_kernel(first, half_ref, codes_ref, scales_ref, spread_ref, *refs):
    out_ref, wide = refs[-2:]
    step = codes_ref.shape[0]

    @pl.when(pl.program_id(0) == 0)
    def _():
        scales = scales_ref[:, first : first + wide.shape[0]].astype(jnp.bfloat16)
        wide[...] = lax.dot_general(
            scales, spread_ref[...], (((0,), (0,)), ((), ())), preferred_element_type=jnp.float32
        )

    rows = pl.ds(pl.multiple_of(pl.program_id(0) * step, step), step)
    out_ref[...] = ((codes_ref[...] - 8).astype(jnp.float32) * wide[rows, :]).astype(jnp.bfloat16)


def dequant(half_id, codes, scales, first, size, earlier=()):
    width = codes.shape[1] // 2
    step = 48
    groups = scales.shape[0]
    spread = np.repeat(np.eye(groups, dtype=np.float32) * CODE_STEP, GROUP, axis=1)
    return pl.pallas_call(
        lambda *refs: dequant_kernel(first, *refs),
        grid_spec=pltpu.PrefetchScalarGridSpec(
            num_scalar_prefetch=1,
            grid=(size // step,),
            in_specs=[
                pl.BlockSpec((step, width), lambda i, half: (first // step + i, half[0])),
                pl.BlockSpec(scales.shape, lambda i, half: (0, 0)),
                pl.BlockSpec((groups, width), lambda i, half: (0, half[0])),
            ]
            + [ANYWHERE] * len(earlier),
            out_specs=pl.BlockSpec((step, width), lambda i, half: (i, 0)),
            scratch_shapes=[pltpu.VMEM((size, width), jnp.float32)],
        ),
        out_shape=jax.ShapeDtypeStruct((size, width), jnp.bfloat16),
        cost_estimate=cost(3),
        name="decode",
    )(half_id, codes, scales, jnp.asarray(spread, dtype=jnp.bfloat16), *earlier)


def level_kernel(sign_ref, own_ref, partner_ref, *refs):
    sign = sign_ref[0].astype(jnp.float32).astype(jnp.bfloat16)
    out_refs = refs[-1:]
    out_refs[0][...] = own_ref[...] * sign + partner_ref[...]


def level_step(value, bit, earlier=()):
    partner = flipped(value, "tp", bit)
    sign = jnp.where(lax.axis_index("tp") & bit == 0, 1, -1).reshape(1)
    size, width = value.shape
    step = next(rows for rows in (112, 96, 80, 64, 48) if size % rows == 0)
    spec = pl.BlockSpec((step, width), lambda i, sign: (i, 0))
    return pl.pallas_call(
        level_kernel,
        grid_spec=pltpu.PrefetchScalarGridSpec(
            num_scalar_prefetch=1,
            grid=(size // step,),
            in_specs=[spec, spec] + [ANYWHERE] * len(earlier),
            out_specs=spec,
        ),
        out_shape=jax.ShapeDtypeStruct(value.shape, jnp.bfloat16),
        cost_estimate=cost(3),
        name="level",
    )(sign, value, partner, *earlier)


def gate_kernel(*refs):
    pass


def gate(value, *earlier):
    return pl.pallas_call(
        gate_kernel,
        in_specs=[ANYWHERE] * (1 + len(earlier)),
        out_specs=ANYWHERE,
        out_shape=jax.ShapeDtypeStruct(value.shape, value.dtype),
        input_output_aliases={0: 0},
        cost_estimate=cost(0),
        name="gate",
    )(value, *earlier)


def project_kernel(chunks, count, half_ref, *refs):
    row_refs, attn_refs, out_side = refs[:count], refs[count : 2 * count], refs[2 * count]
    weights = refs[2 * count + 1 : 2 * count + 1 + 2 * len(chunks)]
    out_ref, total = refs[-2:]
    step = pl.program_id(0)
    steps = pl.num_programs(0)
    rows = row_refs[0].shape[0]
    shards = out_ref.shape[0]
    kept = rows // shards

    def add(parts, sources, first):
        part = jnp.concatenate(parts, axis=0)
        for place, ref in enumerate(sources):
            lanes = slice(place * rows, (place + 1) * rows)
            value = lax.dot_general(part, ref[...], NT, preferred_element_type=jnp.float32)
            total[:, lanes] = value if first else total[:, lanes] + value

    @pl.when(step == 0)
    def _():
        add([out_side[first : first + size, :] for first, size in chunks], attn_refs, True)

    @pl.when(step < steps // 2)
    def _():
        add([ref[...] for ref in weights[0::2]], row_refs, False)

    @pl.when(step >= steps // 2)
    def _():
        add([ref[...] for ref in weights[1::2]], row_refs, False)

    @pl.when(step == steps - 1)
    def _():
        for shard in range(shards):
            for place in range(count):
                first = place * rows + shard * kept
                out_ref[shard, :, place * kept : (place + 1) * kept] = total[
                    :, first : first + kept
                ].astype(jnp.bfloat16)


def project(half_id, shards, row_parts, attn_parts, out_side, weights, chunks, earlier=()):
    count = len(row_parts)
    rows, width = row_parts[0].shape
    steps = 6
    depth = width // steps
    last = steps // 2 - 1
    columns = sum(size for _, size in chunks)
    weight_specs = []
    for _, size in chunks:
        weight_specs += [
            pl.BlockSpec((size, depth), lambda i, h: (0, jnp.minimum(i, last))),
            pl.BlockSpec((size, depth), lambda i, h: (0, jnp.maximum(i - last - 1, 0))),
        ]
    row_spec = pl.BlockSpec((rows, depth), lambda i, h: (0, lax.rem(i + h[0] * (last + 1), steps)))

    def attn_spec(block):
        return pl.BlockSpec((rows, out_side.shape[1]), lambda i, h: (block, 0))

    shape = (shards, columns, count * rows // shards)
    return pl.pallas_call(
        lambda *refs: project_kernel(chunks, count, *refs),
        grid_spec=pltpu.PrefetchScalarGridSpec(
            num_scalar_prefetch=1,
            grid=(steps,),
            in_specs=[row_spec] * count
            + [attn_spec(block) for _, block in attn_parts]
            + [pl.BlockSpec(out_side.shape, lambda i, h: (0, 0))]
            + weight_specs
            + [ANYWHERE] * len(earlier),
            out_specs=pl.BlockSpec(shape, lambda i, h: (0, 0, 0)),
            scratch_shapes=[pltpu.VMEM((columns, count * rows), jnp.float32)],
        ),
        out_shape=jax.ShapeDtypeStruct(shape, jnp.bfloat16),
        compiler_params=pltpu.CompilerParams(vmem_limit_bytes=56 << 20),
        cost_estimate=cost(10),
        name="project",
    )(half_id, *row_parts, *[part for part, _ in attn_parts], out_side, *weights, *earlier)


def turned(head, cosine, signed_sine):
    head = head.astype(jnp.float32)
    return (head * cosine + pltpu.roll(head, HD // 2, 1) * signed_sine).astype(jnp.bfloat16)


def attend_kernel(place_ref, query_ref, cosine_ref, sine_ref, *refs):
    blocks, out_ref = refs[:16], refs[-1]
    rows = query_ref.shape[0]
    half = rows // 2
    heads = query_ref.shape[1] // HD
    key0, value0 = blocks[:2]
    keys = [turned(key0[...], cosine_ref[...], sine_ref[...])]
    values = [value0[...]]
    for block in (1, 2):
        key, value, cosine, sine, cached_key, cached_value = blocks[6 * block - 4 : 6 * block + 2]
        inside = place_ref[pl.program_id(0)] >= block
        keys.append(
            jnp.where(inside, turned(key[...], cosine[...], sine[...]), cached_key[...])
        )
        values.append(jnp.where(inside, value[...], cached_value[...]))
    for part in range(2):
        low = part * half
        here = slice(low, low + half)
        own = slice(0, low + half)
        old = slice(low, rows)
        query = jnp.concatenate(
            [
                turned(
                    query_ref[here, head * HD : (head + 1) * HD],
                    cosine_ref[here, :],
                    sine_ref[here, :],
                )
                for head in range(heads)
            ],
            axis=0,
        )

        def score(block):
            return (
                lax.dot_general(query, block, NT, preferred_element_type=jnp.float32) * SCORE_SCALE
            )

        def places(count, first):
            query_at = lax.broadcasted_iota(jnp.int32, (heads, half, count), 1) + low
            key_at = lax.broadcasted_iota(jnp.int32, (heads, half, count), 2) + first
            shape = (heads * half, count)
            return query_at.reshape(shape), key_at.reshape(shape)

        score0, score1, score2 = score(keys[0][own, :]), score(keys[1]), score(keys[2][old, :])
        query_at, key_at = places(low + half, 0)
        score0 = jnp.where(key_at <= query_at, score0, -jnp.inf)
        query_at, key_at = places(rows - low, low)
        score2 = jnp.where(key_at > query_at, score2, -jnp.inf)
        top = jnp.maximum(
            jnp.max(score0, axis=1, keepdims=True),
            jnp.maximum(
                jnp.max(score1, axis=1, keepdims=True), jnp.max(score2, axis=1, keepdims=True)
            ),
        )
        mass = jnp.zeros_like(top)
        total = jnp.zeros((heads * half, HD), jnp.float32)
        for scores, block in (
            (score0, values[0][own, :]),
            (score1, values[1]),
            (score2, values[2][old, :]),
        ):
            weight = jnp.exp(scores - top)
            mass += jnp.sum(weight, axis=1, keepdims=True)
            total += jnp.dot(
                weight.astype(jnp.bfloat16), block, preferred_element_type=jnp.float32
            )
        total = (total / mass).astype(jnp.bfloat16)
        for head in range(heads):
            out_ref[here, head * HD : (head + 1) * HD] = total[head * half : (head + 1) * half]


def attend(places, kv_heads, cosine, signed_sine, all_shared, ordered, earlier, weight):
    rows = ordered.shape[0] // 2
    first = 2 * kv_heads * HD
    width = all_shared.shape[1] - first
    wide = width // kv_heads
    parts = places.shape[0]

    def pair_specs(row):
        return [
            pl.BlockSpec((rows, HD), lambda t, i, p: (row(p[t]), i)),
            pl.BlockSpec((rows, HD), lambda t, i, p: (row(p[t]), kv_heads + i)),
        ]

    def table_specs(row):
        return [pl.BlockSpec((rows, HD), lambda t, i, p: (row(p[t]), 0))] * 2

    def back(block):
        return lambda place: jnp.maximum(place - block, 0)

    specs = [pl.BlockSpec((rows, wide), lambda t, i, p: (p[t], first // wide + i))]
    specs += table_specs(back(0)) + pair_specs(back(0))
    operands = [all_shared, cosine, signed_sine, all_shared, all_shared]
    for block in (1, 2):
        specs += pair_specs(back(block)) + table_specs(back(block))
        specs += pair_specs(lambda place, block=block: jnp.minimum(place + 2 - block, 1))
        operands += [all_shared, all_shared, cosine, signed_sine, ordered, ordered]
    return pl.pallas_call(
        attend_kernel,
        grid_spec=pltpu.PrefetchScalarGridSpec(
            num_scalar_prefetch=1,
            grid=(parts, kv_heads),
            in_specs=specs + [ANYWHERE] * len(earlier),
            out_specs=pl.BlockSpec((rows, wide), lambda t, i, p: (t, i)),
        ),
        out_shape=jax.ShapeDtypeStruct((parts * rows, width), jnp.bfloat16),
        compiler_params=pltpu.CompilerParams(vmem_limit_bytes=56 << 20),
        cost_estimate=cost(weight),
        name="attend",
    )(places, *operands, *earlier)


def flipped(value, axis, bit):
    return lax.ppermute(value, axis, [(i, i ^ bit) for i in range(lax.axis_size(axis))])


def planned(
    queries, key_value, window_cache, span_start, hidden, down_codes, down_scales, out_weight
):
    half_id = lax.axis_index("group").reshape(1)
    seq_index = lax.axis_index("seq")
    core = seq_index & 1
    side = seq_index >> 1
    tok_rows = queries.shape[0]

    shared = jnp.concatenate([key_value.reshape(tok_rows, -1), queries], axis=1)
    all_shared = lax.all_gather(shared, "seq", axis=0, tiled=True)

    def both_cores(value):
        return [value, flipped(value, "seq", 1)]

    codes = down_codes.T
    out_own = out_weight.T
    (piece_a, piece_c), (piece_b, piece_d) = EARLY, LATE
    piece_a = dequant(half_id, codes, down_scales, *piece_a, (shared,))
    piece_c = dequant(half_id, codes, down_scales, *piece_c, (piece_a,))
    piece_b = dequant(half_id, codes, down_scales, *piece_b, (piece_c,))
    near_hidden = flipped(hidden, "seq", 1)
    rotated = mix_hidden(hidden, piece_b)

    first_pos = gate(span_start, piece_b)[0]
    span = tok_rows * lax.axis_size("seq")
    positions = first_pos + jnp.arange(span, dtype=jnp.int32)
    inv_freq = ROPE_BASE ** (-(2.0 * jnp.arange(HD // 2, dtype=jnp.float32)) / HD)
    angles = positions.astype(jnp.float32)[:, None] * inv_freq[None, :]
    cosine, sine = jnp.cos(angles), jnp.sin(angles)
    cosine = jnp.concatenate([cosine, cosine], axis=1)
    signed_sine = jnp.concatenate([-sine, sine], axis=1)
    cache = window_cache.reshape(WINDOW, -1)
    doubled = jnp.concatenate([cache, cache], axis=0)
    ordered = lax.dynamic_slice_in_dim(doubled, first_pos % WINDOW, WINDOW, 0)

    kv_heads = key_value.shape[2] // HD

    piece_a = level_step(piece_a, 2, (rotated, ordered, cosine, signed_sine))
    piece_c = level_step(piece_c, 1, (piece_a,))
    own_rows = [rotated, mix_hidden(near_hidden, piece_c)]
    def attended_by(flip, earlier, weight):
        places = (seq_index ^ flip).reshape(1)
        return attend(
            places, kv_heads, cosine, signed_sine, all_shared, ordered, earlier, weight
        ), 0

    late_d = dequant(half_id, codes, down_scales, *LATE[1], (own_rows[1],))
    attended = [None] * 4
    attended[0] = attended_by(0, (late_d,), 13)
    piece_b = level_step(piece_b, 2, (piece_c, attended[0][0]))
    attended[2] = attended_by(2, (piece_b,), 13)
    piece_a = level_step(piece_a, 1, (attended[2][0],))
    across_a = flipped(piece_a, "group", 1)
    piece_c = level_step(piece_c, 2, (piece_a,))
    across_c = flipped(piece_c, "group", 1)
    piece_d = level_step(late_d, 1, (piece_c,))
    attended[1] = attended_by(1, (piece_d,), 0)
    attended[3] = attended_by(3, (attended[1][0],), 0)
    piece_b = level_step(piece_b, 1, (attended[3][0], across_a))
    across_b = flipped(piece_b, "group", 1)
    own_attn, far_attn = attended[:2], attended[2:]
    shards = lax.axis_size("tp")

    def reduced(rows, attn, weights, chunks, earlier=(), after=()):
        partial = project(half_id, shards, rows, attn, out_own, weights, chunks, earlier)
        if after:
            partial = gate(partial, *after)
        return lax.psum_scatter(partial, "tp", scatter_dimension=0, tiled=True)[0], partial

    early = [piece_a, across_a, piece_c, across_c]
    own_early, own_done = reduced(own_rows, own_attn, early, EARLY, (piece_b,))
    piece_d = level_step(piece_d, 2, (piece_b, own_done))
    across_d = flipped(piece_d, "group", 1)
    late = [piece_b, across_b, piece_d, across_d]
    far_rows = both_cores(gate(flipped(rotated, "seq", 2), piece_d,across_b))
    far_early, far_done = reduced(far_rows, far_attn, early, EARLY, (across_d,))
    all_late, _ = reduced(
        own_rows + far_rows, own_attn + far_attn, late, LATE, (far_done, own_early), (far_early,)
    )
    kept = tok_rows // shards
    all_early = jnp.concatenate([own_early, far_early], axis=1)
    sums = jnp.concatenate(
        [all_early[:WIDE], all_late[: HALF - WIDE], all_early[WIDE:], all_late[HALF - WIDE :]],
        axis=0,
    )
    strips = [sums[:, i * kept : (i + 1) * kept] for i in range(4)]
    strips = strips[:1] + [flipped(strips[i], "seq", i) for i in (1, 2, 3)]
    strips = [jnp.where(core == 0, strips[i], strips[i ^ 1]) for i in range(4)]
    strips = [jnp.where(side == 0, strips[i], strips[i ^ 2]) for i in range(4)]
    return jnp.concatenate(strips, axis=0).T


def solution(mesh):
    return jax.shard_map(
        planned if fits(mesh) else per_device,
        mesh=mesh,
        in_specs=(
            P(("group", "seq"), "tp"),
            P(("group", "seq"), None, "tp"),
            P("group", None, "tp"),
            P("group"),
            P(("group", "seq"), "tp"),
            P("tp", "seq"),
            P("tp", "seq"),
            P("tp", "seq"),
        ),
        out_specs=P(("group", "seq", "tp"), None),
        check_vma=False,
    )
```

```python
import jax
import jax.numpy as jnp
import numpy as np
from jax import lax
from jax.experimental import pallas as pl
from jax.experimental.pallas import tpu as pltpu
from jax.sharding import PartitionSpec as P

HD = 128
WINDOW = 1024
GROUP = 128


ROPE_BASE = 10000.0
SCORE_SCALE = 168.0 ** (-0.5)
CODE_STEP = 2.0 ** (-14)
INV_ROOT = 1344.0 ** (-0.5)


def shifted(value, axis, steps):
    count = lax.axis_size(axis)
    first, last = (max(0, -steps), min(count, count - steps))
    return lax.ppermute(value, axis, [(source, source + steps) for source in range(first, last)])


def swapped(x, axis, stride):
    return lax.ppermute(x, axis, [(i, i ^ 1 << stride) for i in range(lax.axis_size(axis))])


def bit_total(value_now):
    return (value_now & 1) + (value_now >> 1 & 1) + (value_now >> 2 & 1)


def build_tables():
    prime_order = 167
    residues = set((value_now * value_now % prime_order for value_now in range(1, prime_order)))
    legendre = [0] + [1 if value_now in residues else -1 for value_now in range(1, prime_order)]
    paley_table = np.eye(prime_order + 1)
    paley_table[0, 1:] += 1.0
    paley_table[1:, 0] -= 1.0
    for row_index in range(prime_order):
        for col_index in range(prime_order):
            paley_table[row_index + 1, col_index + 1] += legendre[
                (col_index - row_index) % prime_order
            ]
    sylvester = np.array(
        [
            [(-1.0) ** bit_total(left_bit & right_bit) for right_bit in range(8)]
            for left_bit in range(8)
        ]
    )
    return (paley_table, sylvester)


def rotary(values, cosine, sine_part):
    half_dim = values.shape[-1] // 2
    first_half = values[..., :half_dim]
    second_half = values[..., half_dim:]
    return jnp.concatenate(
        [
            first_half * cosine - second_half * sine_part,
            second_half * cosine + first_half * sine_part,
        ],
        axis=-1,
    )


def section_pairs(blocks_now, section_level):
    row_count, block_count, width_cols = blocks_now.shape
    paired = blocks_now.reshape(
        row_count, block_count >> section_level + 1, 2, 1 << section_level, width_cols
    ).astype(jnp.float32)
    upper_half = paired[:, :, 0]
    lower_half = paired[:, :, 1]
    mixed = jnp.stack([upper_half + lower_half, upper_half - lower_half], axis=2)
    return mixed.astype(jnp.bfloat16).reshape(row_count, block_count, width_cols)


def per_device(
    queries, key_value, window_cache, span_start, hidden, down_codes, down_scales, out_weight
):
    tok_rows = queries.shape[0]
    tp_count = lax.axis_size("tp")
    seq_index = lax.axis_index("seq")
    tp_index = lax.axis_index("tp")
    heads_dev = queries.shape[1] // HD
    kv_dev = key_value.shape[2] // HD
    group_size = heads_dev // kv_dev
    first_pos = span_start[0]
    positions = first_pos + seq_index * tok_rows + jnp.arange(tok_rows, dtype=jnp.int32)
    inv_freq = ROPE_BASE ** (-(2.0 * jnp.arange(HD // 2, dtype=jnp.float32)) / HD)
    angles = positions.astype(jnp.float32)[:, None] * inv_freq[None, :]
    cosine = jnp.cos(angles)[:, None, :]
    sine_part = jnp.sin(angles)[:, None, :]
    query_rot = rotary(
        queries.reshape(tok_rows, heads_dev, HD).astype(jnp.float32), cosine, sine_part
    ).astype(jnp.bfloat16)
    key_rot = rotary(
        key_value[:, 0].reshape(tok_rows, kv_dev, HD).astype(jnp.float32), cosine, sine_part
    ).astype(jnp.bfloat16)
    own_pairs = jnp.stack([key_rot.reshape(tok_rows, kv_dev * HD), key_value[:, 1]], axis=1)
    reach_blocks = WINDOW // tok_rows
    earlier = []
    moving = own_pairs
    for hop_count in range(reach_blocks):
        moving = shifted(moving, "seq", 1)
        earlier.insert(0, moving)
    halo_rows = jnp.concatenate(earlier, axis=0)
    doubled = jnp.concatenate([window_cache, window_cache], axis=0)
    ordered = lax.dynamic_slice_in_dim(doubled, first_pos % WINDOW, WINDOW, 0)
    padded_cache = jnp.concatenate([ordered, jnp.zeros_like(ordered)], axis=0)
    from_cache = lax.dynamic_slice_in_dim(
        padded_cache, jnp.minimum(seq_index * tok_rows, WINDOW), WINDOW, 0
    )
    halo_rows = halo_rows + from_cache
    all_rows = jnp.concatenate([halo_rows, own_pairs], axis=0)
    key_count = all_rows.shape[0]
    key_rows = all_rows[:, 0].reshape(key_count, kv_dev, HD)
    value_rows = all_rows[:, 1].reshape(key_count, kv_dev, HD)
    grouped = query_rot.reshape(tok_rows, kv_dev, group_size, HD)
    scores = (
        jnp.einsum("qkgd,skd->kgqs", grouped, key_rows, preferred_element_type=jnp.float32)
        * SCORE_SCALE
    )
    query_ids = jnp.arange(tok_rows)[:, None]
    key_ids = jnp.arange(key_count)[None, :]
    allowed = (key_ids > query_ids) & (key_ids <= query_ids + WINDOW)
    scores = jnp.where(allowed, scores, -jnp.inf)
    top_score = jnp.max(scores, axis=-1, keepdims=True)
    weights_soft = jnp.exp(scores - top_score)
    weights_soft = (weights_soft / jnp.sum(weights_soft, axis=-1, keepdims=True)).astype(
        jnp.bfloat16
    )
    attended = jnp.einsum(
        "kgqs,skd->qkgd", weights_soft, value_rows, preferred_element_type=jnp.float32
    )
    attended = attended.astype(jnp.bfloat16).reshape(tok_rows, heads_dev * HD)
    paley_np, sylvester_np = build_tables()
    paley_table = jnp.asarray(paley_np, dtype=jnp.bfloat16)
    sylvester = jnp.asarray(sylvester_np, dtype=jnp.float32)
    local_blocks = hidden.shape[1] // 1344
    local_levels = local_blocks.bit_length() - 1
    parts_now = hidden.reshape(tok_rows, local_blocks, 8, 168)
    mixed = jnp.einsum("nbac,cd->nbad", parts_now, paley_table, preferred_element_type=jnp.float32)
    mixed = (
        jnp.einsum("nbad,ae->nbed", mixed, sylvester, precision=lax.Precision.HIGHEST) * INV_ROOT
    )
    blocks_now = mixed.reshape(tok_rows, local_blocks, 1344).astype(jnp.bfloat16)
    for section_level in range(local_levels):
        blocks_now = section_pairs(blocks_now, section_level)
    for bit_index in range(tp_count.bit_length() - 1):
        partner = swapped(blocks_now, "tp", bit_index)
        high_side = jnp.right_shift(tp_index, bit_index) % 2
        own_values = blocks_now.astype(jnp.float32)
        other_values = partner.astype(jnp.float32)
        blocks_now = jnp.where(
            high_side == 0, own_values + other_values, other_values - own_values
        ).astype(jnp.bfloat16)
    rotated = blocks_now.reshape(tok_rows, local_blocks * 1344)
    joined = jnp.concatenate([rotated, attended], axis=1)
    group_count = down_scales.shape[0]
    col_count = down_codes.shape[1]
    down_weight = (
        (down_codes.reshape(group_count, GROUP, col_count) - 8) * down_scales[:, None, :]
    ).astype(jnp.float32) * CODE_STEP
    down_rows = down_weight.astype(jnp.bfloat16).reshape(group_count * GROUP, col_count)
    stacked = jnp.concatenate([down_rows, out_weight], axis=0)
    partials = jnp.dot(
        joined,
        lax.all_gather(stacked, "seq", axis=1, tiled=True),
        preferred_element_type=jnp.float32,
    )
    layer_update = lax.psum_scatter(
        partials.astype(jnp.bfloat16), "tp", scatter_dimension=0, tiled=True
    )
    return layer_update


PIECE = 672
SHIFT = 96
WINDOWED = PIECE + SHIFT
HALF = 336
WIDE = 192
EARLY = ((0, WIDE), (HALF, WIDE))
LATE = ((WIDE, HALF - WIDE), (HALF + WIDE, HALF - WIDE))
NT = (((1,), (1,)), ((), ()))
EXPONENT = SCORE_SCALE / float(np.log(2.0))
ANYWHERE = pl.BlockSpec(memory_space=pl.ANY)


def cost(microseconds):
    return pl.CostEstimate(
        flops=1 + int(microseconds * 1.15e9), bytes_accessed=1, transcendentals=0
    )


def fits(mesh):
    return dict(mesh.shape) == {"group": 2, "seq": 4, "tp": 4}


def mix_tables():
    paley_np, sylvester_np = build_tables()
    table = np.zeros((WINDOWED + SHIFT, WINDOWED), np.float32)
    table[SHIFT : SHIFT + PIECE, :PIECE] = np.kron(sylvester_np[:4, :4], paley_np)
    return jnp.asarray(table, dtype=jnp.bfloat16)


def mix_kernel(hidden_ref, table_ref, *refs):
    out_ref = refs[-1]
    rows = hidden_ref.shape[0]
    pair = 4 * PIECE
    pieces = []
    for place in range(4):
        shift = place * PIECE % 128
        first = place * PIECE - shift
        stacked = jnp.concatenate(
            [
                hidden_ref[:, start + first : start + first + WINDOWED] for start in (0, pair)
            ],
            axis=0,
        )
        table = table_ref[SHIFT - shift : SHIFT - shift + WINDOWED, :]
        pieces.append(jnp.dot(stacked, table, preferred_element_type=jnp.float32) * INV_ROOT)
    for bit in (1, 2):
        pieces = [
            pieces[i] + pieces[i ^ bit] if i & bit == 0 else pieces[i ^ bit] - pieces[i]
            for i in range(4)
        ]
    for half in range(2):
        carried = None
        for place in range(4):
            upper, lower = pieces[place][:rows], pieces[place][rows:]
            value = upper + lower if half == 0 else upper - lower
            shift = place * PIECE % 128
            first = half * pair + place * PIECE - shift
            if shift:
                value = pltpu.roll(value, shift, 1)
                value = jnp.concatenate([value[:, :128] + carried, value[:, 128:]], axis=1)
            keep = WINDOWED if place == 3 else WINDOWED - 128
            out_ref[:, first : first + keep] = value[:, :keep].astype(jnp.bfloat16)
            carried = value[:, keep:]


def mix_hidden(hidden, *earlier):
    rows, width = hidden.shape
    step = 256
    return pl.pallas_call(
        mix_kernel,
        grid=(rows // step,),
        in_specs=[
            pl.BlockSpec((step, width), lambda i: (i, 0)),
            pl.BlockSpec((WINDOWED + SHIFT, WINDOWED), lambda i: (0, 0)),
        ]
        + [ANYWHERE] * len(earlier),
        out_specs=pl.BlockSpec((step, width), lambda i: (i, 0)),
        out_shape=jax.ShapeDtypeStruct((rows, width), jnp.bfloat16),
        compiler_params=pltpu.CompilerParams(vmem_limit_bytes=56 << 20),
        cost_estimate=cost(16),
        name="mix",
    )(hidden, mix_tables(), *earlier)


def dequant_kernel(first, half_ref, codes_ref, scales_ref, spread_ref, *refs):
    out_ref, wide = refs[-2:]
    step = codes_ref.shape[0]

    @pl.when(pl.program_id(0) == 0)
    def _():
        scales = scales_ref[:, first : first + wide.shape[0]].astype(jnp.bfloat16)
        wide[...] = lax.dot_general(
            scales, spread_ref[...], (((0,), (0,)), ((), ())), preferred_element_type=jnp.float32
        )

    rows = pl.ds(pl.multiple_of(pl.program_id(0) * step, step), step)
    out_ref[...] = ((codes_ref[...] - 8).astype(jnp.float32) * wide[rows, :]).astype(jnp.bfloat16)


def dequant(half_id, codes, scales, first, size, earlier=()):
    width = codes.shape[1] // 2
    step = next(rows for rows in (112, 96, 48) if first % rows == size % rows == 0)
    groups = scales.shape[0]
    spread = np.repeat(np.eye(groups, dtype=np.float32) * CODE_STEP, GROUP, axis=1)
    return pl.pallas_call(
        lambda *refs: dequant_kernel(first, *refs),
        grid_spec=pltpu.PrefetchScalarGridSpec(
            num_scalar_prefetch=1,
            grid=(size // step,),
            in_specs=[
                pl.BlockSpec((step, width), lambda i, half: (first // step + i, half[0])),
                pl.BlockSpec(scales.shape, lambda i, half: (0, 0)),
                pl.BlockSpec((groups, width), lambda i, half: (0, half[0])),
            ]
            + [ANYWHERE] * len(earlier),
            out_specs=pl.BlockSpec((step, width), lambda i, half: (i, 0)),
            scratch_shapes=[pltpu.VMEM((size, width), jnp.float32)],
        ),
        out_shape=jax.ShapeDtypeStruct((size, width), jnp.bfloat16),
        cost_estimate=cost(3),
        name="decode",
    )(half_id, codes, scales, jnp.asarray(spread, dtype=jnp.bfloat16), *earlier)


def level_kernel(sign_ref, own_ref, partner_ref, *refs):
    sign = sign_ref[0].astype(jnp.float32).astype(jnp.bfloat16)
    out_refs = refs[-1:]
    out_refs[0][...] = own_ref[...] * sign + partner_ref[...]


def level_step(value, bit, earlier=()):
    partner = flipped(value, "tp", bit)
    sign = jnp.where(lax.axis_index("tp") & bit == 0, 1, -1).reshape(1)
    size, width = value.shape
    step = next(rows for rows in (112, 96, 80, 64, 48) if size % rows == 0)
    spec = pl.BlockSpec((step, width), lambda i, sign: (i, 0))
    return pl.pallas_call(
        level_kernel,
        grid_spec=pltpu.PrefetchScalarGridSpec(
            num_scalar_prefetch=1,
            grid=(size // step,),
            in_specs=[spec, spec] + [ANYWHERE] * len(earlier),
            out_specs=spec,
        ),
        out_shape=jax.ShapeDtypeStruct(value.shape, jnp.bfloat16),
        cost_estimate=cost(3),
        name="level",
    )(sign, value, partner, *earlier)


def gate_kernel(*refs):
    pass


def gate(value, *earlier):
    return pl.pallas_call(
        gate_kernel,
        in_specs=[ANYWHERE] * (1 + len(earlier)),
        out_specs=ANYWHERE,
        out_shape=jax.ShapeDtypeStruct(value.shape, value.dtype),
        input_output_aliases={0: 0},
        cost_estimate=cost(0),
        name="gate",
    )(value, *earlier)


def project_kernel(chunks, count, place_ref, *refs):
    row_refs, attn_refs, out_side = refs[:count], refs[count : 2 * count], refs[2 * count]
    weights = refs[2 * count + 1 : 2 * count + 1 + 2 * len(chunks)]
    out_ref, total = refs[-2:]
    step = pl.program_id(0)
    steps = pl.num_programs(0)
    rows = row_refs[0].shape[0]
    shards = out_ref.shape[0]
    kept = rows // shards

    def add(parts, sources, first):
        part = jnp.concatenate(parts, axis=0)
        for place, ref in enumerate(sources):
            lanes = slice(place * rows, (place + 1) * rows)
            value = lax.dot_general(part, ref[...], NT, preferred_element_type=jnp.float32)
            total[:, lanes] = value if first else total[:, lanes] + value

    @pl.when(step == 0)
    def _():
        add([out_side[first : first + size, :] for first, size in chunks], attn_refs, True)

    @pl.when(step < steps // 2)
    def _():
        add([ref[...] for ref in weights[0::2]], row_refs, False)

    @pl.when(step >= steps // 2)
    def _():
        add([ref[...] for ref in weights[1::2]], row_refs, False)

    @pl.when(step == steps - 1)
    def _():
        for shard in range(shards):
            for place in range(count):
                first = place * rows + shard * kept
                out_ref[shard, :, place * kept : (place + 1) * kept] = total[
                    :, first : first + kept
                ].astype(jnp.bfloat16)


def project(place, shards, row_parts, attn_parts, out_side, weights, chunks, earlier=()):
    count = len(row_parts)
    rows, width = row_parts[0].shape
    steps = 6
    depth = width // steps
    last = steps // 2 - 1
    columns = sum(size for _, size in chunks)
    weight_specs = []
    for _, size in chunks:
        weight_specs += [
            pl.BlockSpec((size, depth), lambda i, h: (0, jnp.minimum(i, last))),
            pl.BlockSpec((size, depth), lambda i, h: (0, jnp.maximum(i - last - 1, 0))),
        ]
    row_spec = pl.BlockSpec((rows, depth), lambda i, h: (0, lax.rem(i + h[0] * (last + 1), steps)))

    def attn_spec(part, flip):
        return pl.BlockSpec(
            (rows, part.shape[1]), lambda i, h: (0 if flip is None else h[1] ^ flip, 0)
        )

    shape = (shards, columns, count * rows // shards)
    return pl.pallas_call(
        lambda *refs: project_kernel(chunks, count, *refs),
        grid_spec=pltpu.PrefetchScalarGridSpec(
            num_scalar_prefetch=1,
            grid=(steps,),
            in_specs=[row_spec] * count
            + [attn_spec(*part) for part in attn_parts]
            + [pl.BlockSpec(out_side.shape, lambda i, h: (0, 0))]
            + weight_specs
            + [ANYWHERE] * len(earlier),
            out_specs=pl.BlockSpec(shape, lambda i, h: (0, 0, 0)),
            scratch_shapes=[pltpu.VMEM((columns, count * rows), jnp.float32)],
        ),
        out_shape=jax.ShapeDtypeStruct(shape, jnp.bfloat16),
        compiler_params=pltpu.CompilerParams(vmem_limit_bytes=56 << 20),
        cost_estimate=cost(10),
        name="project",
    )(place, *row_parts, *[part for part, _ in attn_parts], out_side, *weights, *earlier)


def turned(head, cosine, signed_sine):
    head = head.astype(jnp.float32)
    return (head * cosine + pltpu.roll(head, HD // 2, 1) * signed_sine).astype(jnp.bfloat16)


def attend_kernel(place_ref, query_ref, cosine_ref, sine_ref, *refs):
    blocks, out_ref = refs[:16], refs[-1]
    rows = query_ref.shape[0]
    half = rows // 2
    heads = query_ref.shape[1] // HD
    key0, value0 = blocks[:2]
    keys = [turned(key0[...], cosine_ref[...], sine_ref[...])]
    values = [value0[...]]
    for block in (1, 2):
        key, value, cosine, sine, cached_key, cached_value = blocks[6 * block - 4 : 6 * block + 2]
        inside = place_ref[0] >= block
        keys.append(
            jnp.where(inside, turned(key[...], cosine[...], sine[...]), cached_key[...])
        )
        values.append(jnp.where(inside, value[...], cached_value[...]))
    for part in range(2):
        low = part * half
        here = slice(low, low + half)
        own = slice(0, low + half)
        old = slice(low, rows)
        query = jnp.concatenate(
            [
                turned(
                    query_ref[here, head * HD : (head + 1) * HD],
                    cosine_ref[here, :],
                    sine_ref[here, :],
                )
                for head in range(heads)
            ],
            axis=0,
        )

        def score(block):
            return lax.dot_general(query, block, NT, preferred_element_type=jnp.float32)

        def places(count, first):
            query_at = lax.broadcasted_iota(jnp.int32, (heads, half, count), 1) + low
            key_at = lax.broadcasted_iota(jnp.int32, (heads, half, count), 2) + first
            shape = (heads * half, count)
            return query_at.reshape(shape), key_at.reshape(shape)

        score0, score1, score2 = score(keys[0][own, :]), score(keys[1]), score(keys[2][old, :])
        query_at, key_at = places(low + half, 0)
        score0 = jnp.where(key_at <= query_at, score0, -jnp.inf)
        query_at, key_at = places(rows - low, low)
        score2 = jnp.where(key_at > query_at, score2, -jnp.inf)
        top = jnp.maximum(
            jnp.max(score0, axis=1, keepdims=True),
            jnp.maximum(
                jnp.max(score1, axis=1, keepdims=True), jnp.max(score2, axis=1, keepdims=True)
            ),
        )
        top = top * EXPONENT
        total = jnp.zeros((heads * half, 2 * HD), jnp.float32)
        for scores, block in (
            (score0, values[0][own, :]),
            (score1, values[1]),
            (score2, values[2][old, :]),
        ):
            weight = jnp.exp2(scores * EXPONENT - top).astype(jnp.bfloat16)
            block = jnp.concatenate([block, jnp.ones_like(block)], axis=1)
            total += jnp.dot(weight, block, preferred_element_type=jnp.float32)
        total = (total[:, :HD] / total[:, HD:]).astype(jnp.bfloat16)
        for head in range(heads):
            out_ref[here, head * HD : (head + 1) * HD] = total[head * half : (head + 1) * half]


def attend(places, queries, cosine, signed_sine, all_pairs, ordered, earlier, weight):
    rows = ordered.shape[0] // 2
    width = queries.shape[1]
    kv_heads = all_pairs.shape[1] // (2 * HD)
    wide = width // kv_heads
    gathered = queries.shape[0] > rows

    def pair_specs(row):
        return [
            pl.BlockSpec((rows, HD), lambda i, p: (row(p[0]), i)),
            pl.BlockSpec((rows, HD), lambda i, p: (row(p[0]), kv_heads + i)),
        ]

    def table_specs(row):
        return [pl.BlockSpec((rows, HD), lambda i, p: (row(p[0]), 0))] * 2

    def back(block):
        return lambda place: jnp.maximum(place - block, 0)

    specs = [pl.BlockSpec((rows, wide), lambda i, p: (p[0] if gathered else 0, i))]
    specs += table_specs(back(0)) + pair_specs(back(0))
    operands = [queries, cosine, signed_sine, all_pairs, all_pairs]
    for block in (1, 2):
        specs += pair_specs(back(block)) + table_specs(back(block))
        specs += pair_specs(lambda place, block=block: jnp.minimum(place + 2 - block, 1))
        operands += [all_pairs, all_pairs, cosine, signed_sine, ordered, ordered]
    return pl.pallas_call(
        attend_kernel,
        grid_spec=pltpu.PrefetchScalarGridSpec(
            num_scalar_prefetch=1,
            grid=(kv_heads,),
            in_specs=specs + [ANYWHERE] * len(earlier),
            out_specs=pl.BlockSpec((rows, wide), lambda i, p: (0, i)),
        ),
        out_shape=jax.ShapeDtypeStruct((rows, width), jnp.bfloat16),
        compiler_params=pltpu.CompilerParams(vmem_limit_bytes=56 << 20),
        cost_estimate=cost(weight),
        name="attend",
    )(places, *operands, *earlier)


def flipped(value, axis, bit):
    return lax.ppermute(value, axis, [(i, i ^ bit) for i in range(lax.axis_size(axis))])


def planned(
    queries, key_value, window_cache, span_start, hidden, down_codes, down_scales, out_weight
):
    half_id = lax.axis_index("group").reshape(1)
    seq_index = lax.axis_index("seq")
    core = seq_index & 1
    side = seq_index >> 1
    tok_rows = queries.shape[0]

    pairs = key_value.reshape(tok_rows, -1)
    all_pairs = lax.all_gather(pairs, "seq", axis=0, tiled=True)

    def both_cores(value):
        return [value, flipped(value, "seq", 1)]

    codes = down_codes.T
    out_own = out_weight.T
    (piece_a, piece_c), (piece_b, piece_d) = EARLY, LATE
    piece_a = dequant(half_id, codes, down_scales, *piece_a)
    piece_c = dequant(half_id, codes, down_scales, *piece_c, (piece_a, pairs))
    near_queries = flipped(queries, "seq", 1)
    piece_b = dequant(half_id, codes, down_scales, *piece_b, (piece_c, near_queries))
    near_hidden = flipped(hidden, "seq", 1)
    rotated = mix_hidden(hidden, piece_b)

    first_pos = gate(span_start, piece_b)[0]
    span = tok_rows * lax.axis_size("seq")
    positions = first_pos + jnp.arange(span, dtype=jnp.int32)
    inv_freq = ROPE_BASE ** (-(2.0 * jnp.arange(HD // 2, dtype=jnp.float32)) / HD)
    angles = positions.astype(jnp.float32)[:, None] * inv_freq[None, :]
    cosine, sine = jnp.cos(angles), jnp.sin(angles)
    cosine = jnp.concatenate([cosine, cosine], axis=1)
    signed_sine = jnp.concatenate([-sine, sine], axis=1)
    cache = window_cache.reshape(WINDOW, -1)
    doubled = jnp.concatenate([cache, cache], axis=0)
    ordered = lax.dynamic_slice_in_dim(doubled, first_pos % WINDOW, WINDOW, 0)


    piece_a = level_step(piece_a, 2, (rotated, ordered, cosine, signed_sine))
    piece_c = level_step(piece_c, 1, (piece_a,))


    def attended_by(flip, rows, earlier, weight):
        places = (seq_index ^ flip).reshape(1)
        return attend(places, rows, cosine, signed_sine, all_pairs, ordered, earlier, weight)

    attended = attended_by(0, queries, (piece_c,), 13)
    all_attended = lax.all_gather(attended, "seq", axis=0, tiled=True)
    late_d = dequant(half_id, codes, down_scales, *LATE[1], (attended,))
    own_rows = [rotated, mix_hidden(near_hidden, late_d)]
    piece_b = level_step(piece_b, 2, (piece_c, own_rows[1]))
    piece_a = level_step(piece_a, 1, (piece_b,))
    across_a = flipped(piece_a, "group", 1)
    piece_c = level_step(piece_c, 2, (piece_a,))
    across_c = flipped(piece_c, "group", 1)
    piece_d = level_step(late_d, 1, (piece_c,))
    near_attended = attended_by(1, near_queries, (piece_d,), 0)
    piece_b = level_step(piece_b, 1, (near_attended, across_a))
    across_b = flipped(piece_b, "group", 1)
    place = jnp.stack([half_id[0], seq_index])
    own_attn = [(attended, None), (near_attended, None)]
    far_attn = [(all_attended, 2), (all_attended, 3)]
    shards = lax.axis_size("tp")

    def reduced(rows, attn, weights, chunks, earlier=(), after=()):
        partial = project(place, shards, rows, attn, out_own, weights, chunks, earlier)
        if after:
            partial = gate(partial, *after)
        return lax.psum_scatter(partial, "tp", scatter_dimension=0, tiled=True)[0], partial

    early = [piece_a, across_a, piece_c, across_c]
    own_early, own_done = reduced(own_rows, own_attn, early, EARLY, (piece_b,))
    piece_d = level_step(piece_d, 2, (piece_b, own_done,across_b))
    across_d = flipped(piece_d, "group", 1)
    far_rows = both_cores(gate(flipped(rotated, "seq", 2), piece_d))
    late = [piece_b, across_b, piece_d, across_d]
    far_early, far_done = reduced(far_rows, far_attn, early, EARLY, (piece_d,))
    all_late, _ = reduced(
        own_rows + far_rows, own_attn + far_attn, late, LATE, (far_done, own_early), (far_early,)
    )
    kept = tok_rows // shards

    def handed_out(sums):
        strips = [sums[:, i * kept : (i + 1) * kept] for i in range(4)]
        return strips[:1] + [flipped(strips[i], "seq", i) for i in (1, 2, 3)]

    early_strips = handed_out(jnp.concatenate([own_early, far_early], axis=1))
    late_strips = handed_out(all_late)
    wide, rest = WIDE, HALF - WIDE
    strips = [
        jnp.concatenate([x[:wide], y[:rest], x[wide:], y[rest:]], axis=0)
        for x, y in zip(early_strips, late_strips)
    ]
    strips = [jnp.where(core == 0, strips[i], strips[i ^ 1]) for i in range(4)]
    strips = [jnp.where(side == 0, strips[i], strips[i ^ 2]) for i in range(4)]
    return jnp.concatenate(strips, axis=0).T


def solution(mesh):
    return jax.shard_map(
        planned if fits(mesh) else per_device,
        mesh=mesh,
        in_specs=(
            P(("group", "seq"), "tp"),
            P(("group", "seq"), None, "tp"),
            P("group", None, "tp"),
            P("group"),
            P(("group", "seq"), "tp"),
            P("tp", "seq"),
            P("tp", "seq"),
            P("tp", "seq"),
        ),
        out_specs=P(("group", "seq", "tp"), None),
        check_vma=False,
    )
```

```python
import jax
import jax.numpy as jnp
import numpy as np
from jax import lax
from jax.experimental import pallas as pl
from jax.experimental.pallas import tpu as pltpu
from jax.sharding import PartitionSpec as P

HD = 128
WINDOW = 1024
GROUP = 128


ROPE_BASE = 10000.0
SCORE_SCALE = 168.0 ** (-0.5)
CODE_STEP = 2.0 ** (-14)
INV_ROOT = 1344.0 ** (-0.5)


def shifted(value, axis, steps):
    count = lax.axis_size(axis)
    first, last = (max(0, -steps), min(count, count - steps))
    return lax.ppermute(value, axis, [(source, source + steps) for source in range(first, last)])


def swapped(x, axis, stride):
    return lax.ppermute(x, axis, [(i, i ^ 1 << stride) for i in range(lax.axis_size(axis))])


def bit_total(value_now):
    return (value_now & 1) + (value_now >> 1 & 1) + (value_now >> 2 & 1)


def build_tables():
    prime_order = 167
    residues = set((value_now * value_now % prime_order for value_now in range(1, prime_order)))
    legendre = [0] + [1 if value_now in residues else -1 for value_now in range(1, prime_order)]
    paley_table = np.eye(prime_order + 1)
    paley_table[0, 1:] += 1.0
    paley_table[1:, 0] -= 1.0
    for row_index in range(prime_order):
        for col_index in range(prime_order):
            paley_table[row_index + 1, col_index + 1] += legendre[
                (col_index - row_index) % prime_order
            ]
    sylvester = np.array(
        [
            [(-1.0) ** bit_total(left_bit & right_bit) for right_bit in range(8)]
            for left_bit in range(8)
        ]
    )
    return (paley_table, sylvester)


def rotary(values, cosine, sine_part):
    half_dim = values.shape[-1] // 2
    first_half = values[..., :half_dim]
    second_half = values[..., half_dim:]
    return jnp.concatenate(
        [
            first_half * cosine - second_half * sine_part,
            second_half * cosine + first_half * sine_part,
        ],
        axis=-1,
    )


def section_pairs(blocks_now, section_level):
    row_count, block_count, width_cols = blocks_now.shape
    paired = blocks_now.reshape(
        row_count, block_count >> section_level + 1, 2, 1 << section_level, width_cols
    ).astype(jnp.float32)
    upper_half = paired[:, :, 0]
    lower_half = paired[:, :, 1]
    mixed = jnp.stack([upper_half + lower_half, upper_half - lower_half], axis=2)
    return mixed.astype(jnp.bfloat16).reshape(row_count, block_count, width_cols)


def per_device(
    queries, key_value, window_cache, span_start, hidden, down_codes, down_scales, out_weight
):
    tok_rows = queries.shape[0]
    tp_count = lax.axis_size("tp")
    seq_index = lax.axis_index("seq")
    tp_index = lax.axis_index("tp")
    heads_dev = queries.shape[1] // HD
    kv_dev = key_value.shape[2] // HD
    group_size = heads_dev // kv_dev
    first_pos = span_start[0]
    positions = first_pos + seq_index * tok_rows + jnp.arange(tok_rows, dtype=jnp.int32)
    inv_freq = ROPE_BASE ** (-(2.0 * jnp.arange(HD // 2, dtype=jnp.float32)) / HD)
    angles = positions.astype(jnp.float32)[:, None] * inv_freq[None, :]
    cosine = jnp.cos(angles)[:, None, :]
    sine_part = jnp.sin(angles)[:, None, :]
    query_rot = rotary(
        queries.reshape(tok_rows, heads_dev, HD).astype(jnp.float32), cosine, sine_part
    ).astype(jnp.bfloat16)
    key_rot = rotary(
        key_value[:, 0].reshape(tok_rows, kv_dev, HD).astype(jnp.float32), cosine, sine_part
    ).astype(jnp.bfloat16)
    own_pairs = jnp.stack([key_rot.reshape(tok_rows, kv_dev * HD), key_value[:, 1]], axis=1)
    reach_blocks = WINDOW // tok_rows
    earlier = []
    moving = own_pairs
    for hop_count in range(reach_blocks):
        moving = shifted(moving, "seq", 1)
        earlier.insert(0, moving)
    halo_rows = jnp.concatenate(earlier, axis=0)
    doubled = jnp.concatenate([window_cache, window_cache], axis=0)
    ordered = lax.dynamic_slice_in_dim(doubled, first_pos % WINDOW, WINDOW, 0)
    padded_cache = jnp.concatenate([ordered, jnp.zeros_like(ordered)], axis=0)
    from_cache = lax.dynamic_slice_in_dim(
        padded_cache, jnp.minimum(seq_index * tok_rows, WINDOW), WINDOW, 0
    )
    halo_rows = halo_rows + from_cache
    all_rows = jnp.concatenate([halo_rows, own_pairs], axis=0)
    key_count = all_rows.shape[0]
    key_rows = all_rows[:, 0].reshape(key_count, kv_dev, HD)
    value_rows = all_rows[:, 1].reshape(key_count, kv_dev, HD)
    grouped = query_rot.reshape(tok_rows, kv_dev, group_size, HD)
    scores = (
        jnp.einsum("qkgd,skd->kgqs", grouped, key_rows, preferred_element_type=jnp.float32)
        * SCORE_SCALE
    )
    query_ids = jnp.arange(tok_rows)[:, None]
    key_ids = jnp.arange(key_count)[None, :]
    allowed = (key_ids > query_ids) & (key_ids <= query_ids + WINDOW)
    scores = jnp.where(allowed, scores, -jnp.inf)
    top_score = jnp.max(scores, axis=-1, keepdims=True)
    weights_soft = jnp.exp(scores - top_score)
    weights_soft = (weights_soft / jnp.sum(weights_soft, axis=-1, keepdims=True)).astype(
        jnp.bfloat16
    )
    attended = jnp.einsum(
        "kgqs,skd->qkgd", weights_soft, value_rows, preferred_element_type=jnp.float32
    )
    attended = attended.astype(jnp.bfloat16).reshape(tok_rows, heads_dev * HD)
    paley_np, sylvester_np = build_tables()
    paley_table = jnp.asarray(paley_np, dtype=jnp.bfloat16)
    sylvester = jnp.asarray(sylvester_np, dtype=jnp.float32)
    local_blocks = hidden.shape[1] // 1344
    local_levels = local_blocks.bit_length() - 1
    parts_now = hidden.reshape(tok_rows, local_blocks, 8, 168)
    mixed = jnp.einsum("nbac,cd->nbad", parts_now, paley_table, preferred_element_type=jnp.float32)
    mixed = (
        jnp.einsum("nbad,ae->nbed", mixed, sylvester, precision=lax.Precision.HIGHEST) * INV_ROOT
    )
    blocks_now = mixed.reshape(tok_rows, local_blocks, 1344).astype(jnp.bfloat16)
    for section_level in range(local_levels):
        blocks_now = section_pairs(blocks_now, section_level)
    for bit_index in range(tp_count.bit_length() - 1):
        partner = swapped(blocks_now, "tp", bit_index)
        high_side = jnp.right_shift(tp_index, bit_index) % 2
        own_values = blocks_now.astype(jnp.float32)
        other_values = partner.astype(jnp.float32)
        blocks_now = jnp.where(
            high_side == 0, own_values + other_values, other_values - own_values
        ).astype(jnp.bfloat16)
    rotated = blocks_now.reshape(tok_rows, local_blocks * 1344)
    joined = jnp.concatenate([rotated, attended], axis=1)
    group_count = down_scales.shape[0]
    col_count = down_codes.shape[1]
    down_weight = (
        (down_codes.reshape(group_count, GROUP, col_count) - 8) * down_scales[:, None, :]
    ).astype(jnp.float32) * CODE_STEP
    down_rows = down_weight.astype(jnp.bfloat16).reshape(group_count * GROUP, col_count)
    stacked = jnp.concatenate([down_rows, out_weight], axis=0)
    partials = jnp.dot(
        joined,
        lax.all_gather(stacked, "seq", axis=1, tiled=True),
        preferred_element_type=jnp.float32,
    )
    layer_update = lax.psum_scatter(
        partials.astype(jnp.bfloat16), "tp", scatter_dimension=0, tiled=True
    )
    return layer_update


PIECE = 672
SHIFT = 96
WINDOWED = PIECE + SHIFT
HALF = 336
WIDE = 192
EARLY = ((0, WIDE), (HALF, WIDE))
LATE = ((WIDE, HALF - WIDE), (HALF + WIDE, HALF - WIDE))
NT = (((1,), (1,)), ((), ()))
EXPONENT = SCORE_SCALE / float(np.log(2.0))
ANYWHERE = pl.BlockSpec(memory_space=pl.ANY)


def cost(microseconds):
    return pl.CostEstimate(
        flops=1 + int(microseconds * 1.15e9), bytes_accessed=1, transcendentals=0
    )


def fits(mesh):
    return dict(mesh.shape) == {"group": 2, "seq": 4, "tp": 4}


def mix_tables():
    paley_np, sylvester_np = build_tables()
    table = np.zeros((WINDOWED + SHIFT, WINDOWED), np.float32)
    table[SHIFT : SHIFT + PIECE, :PIECE] = np.kron(sylvester_np[:4, :4], paley_np)
    return jnp.asarray(table, dtype=jnp.bfloat16)


def mix_kernel(hidden_ref, table_ref, *refs):
    out_ref = refs[-1]
    rows = hidden_ref.shape[0]
    pair = 4 * PIECE
    pieces = []
    for place in range(4):
        shift = place * PIECE % 128
        first = place * PIECE - shift
        stacked = jnp.concatenate(
            [
                hidden_ref[:, start + first : start + first + WINDOWED] for start in (0, pair)
            ],
            axis=0,
        )
        table = table_ref[SHIFT - shift : SHIFT - shift + WINDOWED, :]
        pieces.append(jnp.dot(stacked, table, preferred_element_type=jnp.float32) * INV_ROOT)
    for bit in (1, 2):
        pieces = [
            pieces[i] + pieces[i ^ bit] if i & bit == 0 else pieces[i ^ bit] - pieces[i]
            for i in range(4)
        ]
    for half in range(2):
        carried = None
        for place in range(4):
            upper, lower = pieces[place][:rows], pieces[place][rows:]
            value = upper + lower if half == 0 else upper - lower
            shift = place * PIECE % 128
            first = half * pair + place * PIECE - shift
            if shift:
                value = pltpu.roll(value, shift, 1)
                value = jnp.concatenate([value[:, :128] + carried, value[:, 128:]], axis=1)
            keep = WINDOWED if place == 3 else WINDOWED - 128
            out_ref[:, first : first + keep] = value[:, :keep].astype(jnp.bfloat16)
            carried = value[:, keep:]


def mix_hidden(hidden, *earlier):
    rows, width = hidden.shape
    step = 256
    return pl.pallas_call(
        mix_kernel,
        grid=(rows // step,),
        in_specs=[
            pl.BlockSpec((step, width), lambda i: (i, 0)),
            pl.BlockSpec((WINDOWED + SHIFT, WINDOWED), lambda i: (0, 0)),
        ]
        + [ANYWHERE] * len(earlier),
        out_specs=pl.BlockSpec((step, width), lambda i: (i, 0)),
        out_shape=jax.ShapeDtypeStruct((rows, width), jnp.bfloat16),
        compiler_params=pltpu.CompilerParams(vmem_limit_bytes=56 << 20),
        cost_estimate=cost(16),
        name="mix",
    )(hidden, mix_tables(), *earlier)


def dequant_kernel(first, half_ref, codes_ref, scales_ref, spread_ref, *refs):
    out_ref, wide = refs[-2:]
    step = codes_ref.shape[0]

    @pl.when(pl.program_id(0) == 0)
    def _():
        scales = scales_ref[:, first : first + wide.shape[0]].astype(jnp.bfloat16)
        wide[...] = lax.dot_general(
            scales, spread_ref[...], (((0,), (0,)), ((), ())), preferred_element_type=jnp.float32
        )

    rows = pl.ds(pl.multiple_of(pl.program_id(0) * step, step), step)
    out_ref[...] = ((codes_ref[...] - 8).astype(jnp.float32) * wide[rows, :]).astype(jnp.bfloat16)


def dequant(half_id, codes, scales, first, size, earlier=()):
    width = codes.shape[1] // 2
    step = next(rows for rows in (112, 96, 48) if first % rows == size % rows == 0)
    groups = scales.shape[0]
    spread = np.repeat(np.eye(groups, dtype=np.float32) * CODE_STEP, GROUP, axis=1)
    return pl.pallas_call(
        lambda *refs: dequant_kernel(first, *refs),
        grid_spec=pltpu.PrefetchScalarGridSpec(
            num_scalar_prefetch=1,
            grid=(size // step,),
            in_specs=[
                pl.BlockSpec((step, width), lambda i, half: (first // step + i, half[0])),
                pl.BlockSpec(scales.shape, lambda i, half: (0, 0)),
                pl.BlockSpec((groups, width), lambda i, half: (0, half[0])),
            ]
            + [ANYWHERE] * len(earlier),
            out_specs=pl.BlockSpec((step, width), lambda i, half: (i, 0)),
            scratch_shapes=[pltpu.VMEM((size, width), jnp.float32)],
        ),
        out_shape=jax.ShapeDtypeStruct((size, width), jnp.bfloat16),
        cost_estimate=cost(3),
        name="decode",
    )(half_id, codes, scales, jnp.asarray(spread, dtype=jnp.bfloat16), *earlier)


def level_kernel(sign_ref, own_ref, partner_ref, *refs):
    sign = sign_ref[0].astype(jnp.float32).astype(jnp.bfloat16)
    out_refs = refs[-1:]
    out_refs[0][...] = own_ref[...] * sign + partner_ref[...]


def level_step(value, bit, earlier=()):
    partner = flipped(value, "tp", bit)
    sign = jnp.where(lax.axis_index("tp") & bit == 0, 1, -1).reshape(1)
    size, width = value.shape
    step = next(rows for rows in (112, 96, 80, 64, 48) if size % rows == 0)
    spec = pl.BlockSpec((step, width), lambda i, sign: (i, 0))
    return pl.pallas_call(
        level_kernel,
        grid_spec=pltpu.PrefetchScalarGridSpec(
            num_scalar_prefetch=1,
            grid=(size // step,),
            in_specs=[spec, spec] + [ANYWHERE] * len(earlier),
            out_specs=spec,
        ),
        out_shape=jax.ShapeDtypeStruct(value.shape, jnp.bfloat16),
        cost_estimate=cost(3),
        name="level",
    )(sign, value, partner, *earlier)


def gate_kernel(*refs):
    pass


def gate(value, *earlier):
    return pl.pallas_call(
        gate_kernel,
        in_specs=[ANYWHERE] * (1 + len(earlier)),
        out_specs=ANYWHERE,
        out_shape=jax.ShapeDtypeStruct(value.shape, value.dtype),
        input_output_aliases={0: 0},
        cost_estimate=cost(0),
        name="gate",
    )(value, *earlier)


def project_kernel(chunks, flips, place_ref, *refs):
    count = len(flips)
    row_refs, attn_refs, side_ref = refs[:count], refs[count : 2 * count], refs[2 * count]
    weights = refs[2 * count + 1 : 2 * count + 1 + 2 * len(chunks)]
    out_ref, total, attn, out_side, arrived = refs[-5:]
    step = pl.program_id(0)
    steps = pl.num_programs(0)
    rows = row_refs[0].shape[0]
    shards = out_ref.shape[0]
    kept = rows // shards

    def add(parts, sources, first):
        part = jnp.concatenate(parts, axis=0)
        for place, ref in enumerate(sources):
            lanes = slice(place * rows, (place + 1) * rows)
            value = lax.dot_general(part, ref[...], NT, preferred_element_type=jnp.float32)
            total[:, lanes] = value if first else total[:, lanes] + value

    def fetches():
        yield pltpu.make_async_copy(side_ref, out_side, arrived.at[count])
        for place, flip in enumerate(flips):
            block = 0 if flip is None else place_ref[1] ^ flip
            source = attn_refs[place].at[pl.ds(pl.multiple_of(block * rows, rows), rows), :]
            yield pltpu.make_async_copy(source, attn.at[place], arrived.at[place])

    @pl.when(step == 0)
    def _():
        for fetch in fetches():
            fetch.start()
        add([ref[...] for ref in weights[0::2]], row_refs, True)

    @pl.when((step > 0) & (step < steps // 2))
    def _():
        add([ref[...] for ref in weights[0::2]], row_refs, False)

    @pl.when(step >= steps // 2)
    def _():
        add([ref[...] for ref in weights[1::2]], row_refs, False)

    @pl.when(step == steps - 1)
    def _():
        for fetch in fetches():
            fetch.wait()
        side = [out_side[first : first + size, :] for first, size in chunks]
        add(side, [attn.at[place] for place in range(count)], False)
        for shard in range(shards):
            for place in range(count):
                first = place * rows + shard * kept
                out_ref[shard, :, place * kept : (place + 1) * kept] = total[
                    :, first : first + kept
                ].astype(jnp.bfloat16)


def project(place, shards, row_parts, attn_parts, out_side, weights, chunks, earlier=()):
    count = len(row_parts)
    rows, width = row_parts[0].shape
    steps = 6
    depth = width // steps
    last = steps // 2 - 1
    columns = sum(size for _, size in chunks)
    weight_specs = []
    for _, size in chunks:
        weight_specs += [
            pl.BlockSpec((size, depth), lambda i, h: (0, jnp.minimum(i, last))),
            pl.BlockSpec((size, depth), lambda i, h: (0, jnp.maximum(i - last - 1, 0))),
        ]
    row_spec = pl.BlockSpec((rows, depth), lambda i, h: (0, lax.rem(i + h[0] * (last + 1), steps)))

    shape = (shards, columns, count * rows // shards)
    return pl.pallas_call(
        lambda *refs: project_kernel(chunks, [flip for _, flip in attn_parts], *refs),
        grid_spec=pltpu.PrefetchScalarGridSpec(
            num_scalar_prefetch=1,
            grid=(steps,),
            in_specs=[row_spec] * count
            + [ANYWHERE] * (count + 1)
            + weight_specs
            + [ANYWHERE] * len(earlier),
            out_specs=pl.BlockSpec(shape, lambda i, h: (0, 0, 0)),
            scratch_shapes=[
                pltpu.VMEM((columns, count * rows), jnp.float32),
                pltpu.VMEM((count, rows, out_side.shape[1]), jnp.bfloat16),
                pltpu.VMEM(out_side.shape, jnp.bfloat16),
                pltpu.SemaphoreType.DMA((count + 1,)),
            ],
        ),
        out_shape=jax.ShapeDtypeStruct(shape, jnp.bfloat16),
        compiler_params=pltpu.CompilerParams(vmem_limit_bytes=56 << 20),
        cost_estimate=cost(10),
        name="project",
    )(place, *row_parts, *[part for part, _ in attn_parts], out_side, *weights, *earlier)


def turned(head, cosine, signed_sine):
    head = head.astype(jnp.float32)
    return (head * cosine + pltpu.roll(head, HD // 2, 1) * signed_sine).astype(jnp.bfloat16)


def attend_kernel(place_ref, query_ref, cosine_ref, sine_ref, *refs):
    blocks, out_ref = refs[:16], refs[-1]
    rows = query_ref.shape[0]
    half = rows // 2
    heads = query_ref.shape[1] // HD
    key0, value0 = blocks[:2]
    keys = [turned(key0[...], cosine_ref[...], sine_ref[...])]
    values = [value0[...]]
    for block in (1, 2):
        key, value, cosine, sine, cached_key, cached_value = blocks[6 * block - 4 : 6 * block + 2]
        inside = place_ref[0] >= block
        keys.append(
            jnp.where(inside, turned(key[...], cosine[...], sine[...]), cached_key[...])
        )
        values.append(jnp.where(inside, value[...], cached_value[...]))
    for part in range(2):
        low = part * half
        here = slice(low, low + half)
        own = slice(0, low + half)
        old = slice(low, rows)
        query = jnp.concatenate(
            [
                turned(
                    query_ref[here, head * HD : (head + 1) * HD],
                    cosine_ref[here, :],
                    sine_ref[here, :],
                )
                for head in range(heads)
            ],
            axis=0,
        )

        def score(block):
            return lax.dot_general(query, block, NT, preferred_element_type=jnp.float32)

        def places(count, first):
            query_at = lax.broadcasted_iota(jnp.int32, (heads, half, count), 1) + low
            key_at = lax.broadcasted_iota(jnp.int32, (heads, half, count), 2) + first
            shape = (heads * half, count)
            return query_at.reshape(shape), key_at.reshape(shape)

        score0, score1, score2 = score(keys[0][own, :]), score(keys[1]), score(keys[2][old, :])
        query_at, key_at = places(low + half, 0)
        score0 = jnp.where(key_at <= query_at, score0, -jnp.inf)
        query_at, key_at = places(rows - low, low)
        score2 = jnp.where(key_at > query_at, score2, -jnp.inf)
        top = jnp.maximum(
            jnp.max(score0, axis=1, keepdims=True),
            jnp.maximum(
                jnp.max(score1, axis=1, keepdims=True), jnp.max(score2, axis=1, keepdims=True)
            ),
        )
        top = top * EXPONENT
        total = jnp.zeros((heads * half, 2 * HD), jnp.float32)
        for scores, block in (
            (score0, values[0][own, :]),
            (score1, values[1]),
            (score2, values[2][old, :]),
        ):
            weight = jnp.exp2(scores * EXPONENT - top).astype(jnp.bfloat16)
            block = jnp.concatenate([block, jnp.ones_like(block)], axis=1)
            total += jnp.dot(weight, block, preferred_element_type=jnp.float32)
        total = (total[:, :HD] / total[:, HD:]).astype(jnp.bfloat16)
        for head in range(heads):
            out_ref[here, head * HD : (head + 1) * HD] = total[head * half : (head + 1) * half]


def attend(places, queries, cosine, signed_sine, all_pairs, ordered, earlier, weight):
    rows = ordered.shape[0] // 2
    width = queries.shape[1]
    kv_heads = all_pairs.shape[1] // (2 * HD)
    wide = width // kv_heads
    gathered = queries.shape[0] > rows

    def pair_specs(row):
        return [
            pl.BlockSpec((rows, HD), lambda i, p: (row(p[0]), i)),
            pl.BlockSpec((rows, HD), lambda i, p: (row(p[0]), kv_heads + i)),
        ]

    def table_specs(row):
        return [pl.BlockSpec((rows, HD), lambda i, p: (row(p[0]), 0))] * 2

    def back(block):
        return lambda place: jnp.maximum(place - block, 0)

    specs = [pl.BlockSpec((rows, wide), lambda i, p: (p[0] if gathered else 0, i))]
    specs += table_specs(back(0)) + pair_specs(back(0))
    operands = [queries, cosine, signed_sine, all_pairs, all_pairs]
    for block in (1, 2):
        specs += pair_specs(back(block)) + table_specs(back(block))
        specs += pair_specs(lambda place, block=block: jnp.minimum(place + 2 - block, 1))
        operands += [all_pairs, all_pairs, cosine, signed_sine, ordered, ordered]
    return pl.pallas_call(
        attend_kernel,
        grid_spec=pltpu.PrefetchScalarGridSpec(
            num_scalar_prefetch=1,
            grid=(kv_heads,),
            in_specs=specs + [ANYWHERE] * len(earlier),
            out_specs=pl.BlockSpec((rows, wide), lambda i, p: (0, i)),
        ),
        out_shape=jax.ShapeDtypeStruct((rows, width), jnp.bfloat16),
        compiler_params=pltpu.CompilerParams(vmem_limit_bytes=56 << 20),
        cost_estimate=cost(weight),
        name="attend",
    )(places, *operands, *earlier)


def flipped(value, axis, bit):
    return lax.ppermute(value, axis, [(i, i ^ bit) for i in range(lax.axis_size(axis))])


def planned(
    queries, key_value, window_cache, span_start, hidden, down_codes, down_scales, out_weight
):
    half_id = lax.axis_index("group").reshape(1)
    seq_index = lax.axis_index("seq")
    core = seq_index & 1
    side = seq_index >> 1
    tok_rows = queries.shape[0]

    pairs = key_value.reshape(tok_rows, -1)
    all_pairs = lax.all_gather(pairs, "seq", axis=0, tiled=True)

    def both_cores(value):
        return [value, flipped(value, "seq", 1)]

    codes = down_codes.T
    out_own = out_weight.T
    (piece_a, piece_c), (piece_b, piece_d) = EARLY, LATE
    piece_a = dequant(half_id, codes, down_scales, *piece_a)
    piece_c = dequant(half_id, codes, down_scales, *piece_c, (piece_a, pairs))
    near_queries = flipped(queries, "seq", 1)
    piece_b = dequant(half_id, codes, down_scales, *piece_b, (piece_c, near_queries))
    near_hidden = flipped(hidden, "seq", 1)
    rotated = mix_hidden(hidden, piece_b)

    first_pos = gate(span_start, piece_b)[0]
    span = tok_rows * lax.axis_size("seq")
    positions = first_pos + jnp.arange(span, dtype=jnp.int32)
    inv_freq = ROPE_BASE ** (-(2.0 * jnp.arange(HD // 2, dtype=jnp.float32)) / HD)
    angles = positions.astype(jnp.float32)[:, None] * inv_freq[None, :]
    cosine, sine = jnp.cos(angles), jnp.sin(angles)
    cosine = jnp.concatenate([cosine, cosine], axis=1)
    signed_sine = jnp.concatenate([-sine, sine], axis=1)
    cache = window_cache.reshape(WINDOW, -1)
    doubled = jnp.concatenate([cache, cache], axis=0)
    ordered = lax.dynamic_slice_in_dim(doubled, first_pos % WINDOW, WINDOW, 0)


    piece_a = level_step(piece_a, 2, (rotated, ordered, cosine, signed_sine))
    piece_c = level_step(piece_c, 1, (piece_a,))


    def attended_by(flip, rows, earlier, weight):
        places = (seq_index ^ flip).reshape(1)
        return attend(places, rows, cosine, signed_sine, all_pairs, ordered, earlier, weight)

    attended = attended_by(0, queries, (piece_c,), 13)
    all_attended = lax.all_gather(attended, "seq", axis=0, tiled=True)
    late_d = dequant(half_id, codes, down_scales, *LATE[1], (attended,))
    own_rows = [rotated, mix_hidden(near_hidden, late_d)]
    piece_b = level_step(piece_b, 2, (piece_c, own_rows[1]))
    piece_a = level_step(piece_a, 1, (piece_b,))
    across_a = flipped(piece_a, "group", 1)
    near_attended = attended_by(1, near_queries, (piece_a,), 0)
    piece_c = level_step(piece_c, 2, (near_attended,))
    across_c = flipped(piece_c, "group", 1)
    piece_d = level_step(late_d, 1, (piece_c,))
    piece_b = level_step(piece_b, 1, (piece_d, across_a))
    across_b = flipped(piece_b, "group", 1)
    place = jnp.stack([half_id[0], seq_index])
    own_attn = [(attended, None), (near_attended, None)]
    far_attn = [(all_attended, 2), (all_attended, 3)]
    shards = lax.axis_size("tp")

    def reduced(rows, attn, weights, chunks, earlier=(), after=()):
        partial = project(place, shards, rows, attn, out_own, weights, chunks, earlier)
        if after:
            partial = gate(partial, *after)
        return lax.psum_scatter(partial, "tp", scatter_dimension=0, tiled=True)[0], partial

    early = [piece_a, across_a, piece_c, across_c]
    own_early, own_done = reduced(own_rows, own_attn, early, EARLY, (piece_b,))
    piece_d = level_step(piece_d, 2, (piece_b, own_done,across_b))
    across_d = flipped(piece_d, "group", 1)
    far_rows = both_cores(gate(flipped(rotated, "seq", 2), piece_d))
    late = [piece_b, across_b, piece_d, across_d]
    far_early, far_done = reduced(far_rows, far_attn, early, EARLY, (piece_d,))
    all_late, _ = reduced(
        own_rows + far_rows, own_attn + far_attn, late, LATE, (far_done, own_early), (far_early,)
    )
    kept = tok_rows // shards

    def handed_out(sums):
        strips = [sums[:, i * kept : (i + 1) * kept] for i in range(4)]
        return strips[:1] + [flipped(strips[i], "seq", i) for i in (1, 2, 3)]

    early_strips = handed_out(jnp.concatenate([own_early, far_early], axis=1))
    late_strips = handed_out(all_late)
    wide, rest = WIDE, HALF - WIDE
    strips = [
        jnp.concatenate([x[:wide], y[:rest], x[wide:], y[rest:]], axis=0)
        for x, y in zip(early_strips, late_strips)
    ]
    strips = [jnp.where(core == 0, strips[i], strips[i ^ 1]) for i in range(4)]
    strips = [jnp.where(side == 0, strips[i], strips[i ^ 2]) for i in range(4)]
    return jnp.concatenate(strips, axis=0).T


def solution(mesh):
    return jax.shard_map(
        planned if fits(mesh) else per_device,
        mesh=mesh,
        in_specs=(
            P(("group", "seq"), "tp"),
            P(("group", "seq"), None, "tp"),
            P("group", None, "tp"),
            P("group"),
            P(("group", "seq"), "tp"),
            P("tp", "seq"),
            P("tp", "seq"),
            P("tp", "seq"),
        ),
        out_specs=P(("group", "seq", "tp"), None),
        check_vma=False,
    )
```

```python
import jax
import jax.numpy as jnp
import numpy as np
from jax import lax
from jax.experimental import pallas as pl
from jax.experimental.pallas import tpu as pltpu
from jax.sharding import PartitionSpec as P

HD = 128
WINDOW = 1024
GROUP = 128


ROPE_BASE = 10000.0
SCORE_SCALE = 168.0 ** (-0.5)
CODE_STEP = 2.0 ** (-14)
INV_ROOT = 1344.0 ** (-0.5)


def shifted(value, axis, steps):
    count = lax.axis_size(axis)
    first, last = (max(0, -steps), min(count, count - steps))
    return lax.ppermute(value, axis, [(source, source + steps) for source in range(first, last)])


def swapped(x, axis, stride):
    return lax.ppermute(x, axis, [(i, i ^ 1 << stride) for i in range(lax.axis_size(axis))])


def bit_total(value_now):
    return (value_now & 1) + (value_now >> 1 & 1) + (value_now >> 2 & 1)


def build_tables():
    prime_order = 167
    residues = set((value_now * value_now % prime_order for value_now in range(1, prime_order)))
    legendre = [0] + [1 if value_now in residues else -1 for value_now in range(1, prime_order)]
    paley_table = np.eye(prime_order + 1)
    paley_table[0, 1:] += 1.0
    paley_table[1:, 0] -= 1.0
    for row_index in range(prime_order):
        for col_index in range(prime_order):
            paley_table[row_index + 1, col_index + 1] += legendre[
                (col_index - row_index) % prime_order
            ]
    sylvester = np.array(
        [
            [(-1.0) ** bit_total(left_bit & right_bit) for right_bit in range(8)]
            for left_bit in range(8)
        ]
    )
    return (paley_table, sylvester)


def rotary(values, cosine, sine_part):
    half_dim = values.shape[-1] // 2
    first_half = values[..., :half_dim]
    second_half = values[..., half_dim:]
    return jnp.concatenate(
        [
            first_half * cosine - second_half * sine_part,
            second_half * cosine + first_half * sine_part,
        ],
        axis=-1,
    )


def section_pairs(blocks_now, section_level):
    row_count, block_count, width_cols = blocks_now.shape
    paired = blocks_now.reshape(
        row_count, block_count >> section_level + 1, 2, 1 << section_level, width_cols
    ).astype(jnp.float32)
    upper_half = paired[:, :, 0]
    lower_half = paired[:, :, 1]
    mixed = jnp.stack([upper_half + lower_half, upper_half - lower_half], axis=2)
    return mixed.astype(jnp.bfloat16).reshape(row_count, block_count, width_cols)


def per_device(
    queries, key_value, window_cache, span_start, hidden, down_codes, down_scales, out_weight
):
    tok_rows = queries.shape[0]
    tp_count = lax.axis_size("tp")
    seq_index = lax.axis_index("seq")
    tp_index = lax.axis_index("tp")
    heads_dev = queries.shape[1] // HD
    kv_dev = key_value.shape[2] // HD
    group_size = heads_dev // kv_dev
    first_pos = span_start[0]
    positions = first_pos + seq_index * tok_rows + jnp.arange(tok_rows, dtype=jnp.int32)
    inv_freq = ROPE_BASE ** (-(2.0 * jnp.arange(HD // 2, dtype=jnp.float32)) / HD)
    angles = positions.astype(jnp.float32)[:, None] * inv_freq[None, :]
    cosine = jnp.cos(angles)[:, None, :]
    sine_part = jnp.sin(angles)[:, None, :]
    query_rot = rotary(
        queries.reshape(tok_rows, heads_dev, HD).astype(jnp.float32), cosine, sine_part
    ).astype(jnp.bfloat16)
    key_rot = rotary(
        key_value[:, 0].reshape(tok_rows, kv_dev, HD).astype(jnp.float32), cosine, sine_part
    ).astype(jnp.bfloat16)
    own_pairs = jnp.stack([key_rot.reshape(tok_rows, kv_dev * HD), key_value[:, 1]], axis=1)
    reach_blocks = WINDOW // tok_rows
    earlier = []
    moving = own_pairs
    for hop_count in range(reach_blocks):
        moving = shifted(moving, "seq", 1)
        earlier.insert(0, moving)
    halo_rows = jnp.concatenate(earlier, axis=0)
    doubled = jnp.concatenate([window_cache, window_cache], axis=0)
    ordered = lax.dynamic_slice_in_dim(doubled, first_pos % WINDOW, WINDOW, 0)
    padded_cache = jnp.concatenate([ordered, jnp.zeros_like(ordered)], axis=0)
    from_cache = lax.dynamic_slice_in_dim(
        padded_cache, jnp.minimum(seq_index * tok_rows, WINDOW), WINDOW, 0
    )
    halo_rows = halo_rows + from_cache
    all_rows = jnp.concatenate([halo_rows, own_pairs], axis=0)
    key_count = all_rows.shape[0]
    key_rows = all_rows[:, 0].reshape(key_count, kv_dev, HD)
    value_rows = all_rows[:, 1].reshape(key_count, kv_dev, HD)
    grouped = query_rot.reshape(tok_rows, kv_dev, group_size, HD)
    scores = (
        jnp.einsum("qkgd,skd->kgqs", grouped, key_rows, preferred_element_type=jnp.float32)
        * SCORE_SCALE
    )
    query_ids = jnp.arange(tok_rows)[:, None]
    key_ids = jnp.arange(key_count)[None, :]
    allowed = (key_ids > query_ids) & (key_ids <= query_ids + WINDOW)
    scores = jnp.where(allowed, scores, -jnp.inf)
    top_score = jnp.max(scores, axis=-1, keepdims=True)
    weights_soft = jnp.exp(scores - top_score)
    weights_soft = (weights_soft / jnp.sum(weights_soft, axis=-1, keepdims=True)).astype(
        jnp.bfloat16
    )
    attended = jnp.einsum(
        "kgqs,skd->qkgd", weights_soft, value_rows, preferred_element_type=jnp.float32
    )
    attended = attended.astype(jnp.bfloat16).reshape(tok_rows, heads_dev * HD)
    paley_np, sylvester_np = build_tables()
    paley_table = jnp.asarray(paley_np, dtype=jnp.bfloat16)
    sylvester = jnp.asarray(sylvester_np, dtype=jnp.float32)
    local_blocks = hidden.shape[1] // 1344
    local_levels = local_blocks.bit_length() - 1
    parts_now = hidden.reshape(tok_rows, local_blocks, 8, 168)
    mixed = jnp.einsum("nbac,cd->nbad", parts_now, paley_table, preferred_element_type=jnp.float32)
    mixed = (
        jnp.einsum("nbad,ae->nbed", mixed, sylvester, precision=lax.Precision.HIGHEST) * INV_ROOT
    )
    blocks_now = mixed.reshape(tok_rows, local_blocks, 1344).astype(jnp.bfloat16)
    for section_level in range(local_levels):
        blocks_now = section_pairs(blocks_now, section_level)
    for bit_index in range(tp_count.bit_length() - 1):
        partner = swapped(blocks_now, "tp", bit_index)
        high_side = jnp.right_shift(tp_index, bit_index) % 2
        own_values = blocks_now.astype(jnp.float32)
        other_values = partner.astype(jnp.float32)
        blocks_now = jnp.where(
            high_side == 0, own_values + other_values, other_values - own_values
        ).astype(jnp.bfloat16)
    rotated = blocks_now.reshape(tok_rows, local_blocks * 1344)
    joined = jnp.concatenate([rotated, attended], axis=1)
    group_count = down_scales.shape[0]
    col_count = down_codes.shape[1]
    down_weight = (
        (down_codes.reshape(group_count, GROUP, col_count) - 8) * down_scales[:, None, :]
    ).astype(jnp.float32) * CODE_STEP
    down_rows = down_weight.astype(jnp.bfloat16).reshape(group_count * GROUP, col_count)
    stacked = jnp.concatenate([down_rows, out_weight], axis=0)
    partials = jnp.dot(
        joined,
        lax.all_gather(stacked, "seq", axis=1, tiled=True),
        preferred_element_type=jnp.float32,
    )
    layer_update = lax.psum_scatter(
        partials.astype(jnp.bfloat16), "tp", scatter_dimension=0, tiled=True
    )
    return layer_update


PIECE = 672
SHIFT = 96
WINDOWED = PIECE + SHIFT
HALF = 336
WIDE = 192
EARLY = ((0, WIDE), (HALF, WIDE))
LATE = ((WIDE, HALF - WIDE), (HALF + WIDE, HALF - WIDE))
NT = (((1,), (1,)), ((), ()))
EXPONENT = SCORE_SCALE / float(np.log(2.0))
ANYWHERE = pl.BlockSpec(memory_space=pl.ANY)


def cost(microseconds):
    return pl.CostEstimate(
        flops=1 + int(microseconds * 1.15e9), bytes_accessed=1, transcendentals=0
    )


def fits(mesh):
    return dict(mesh.shape) == {"group": 2, "seq": 4, "tp": 4}


def mix_tables():
    paley_np, sylvester_np = build_tables()
    table = np.zeros((WINDOWED + SHIFT, WINDOWED), np.float32)
    table[SHIFT : SHIFT + PIECE, :PIECE] = np.kron(sylvester_np[:4, :4], paley_np)
    return jnp.asarray(table, dtype=jnp.bfloat16)


def mix_kernel(hidden_ref, table_ref, *refs):
    out_ref = refs[-1]
    rows = hidden_ref.shape[0]
    pair = 4 * PIECE
    pieces = []
    for place in range(4):
        shift = place * PIECE % 128
        first = place * PIECE - shift
        stacked = jnp.concatenate(
            [
                hidden_ref[:, start + first : start + first + WINDOWED] for start in (0, pair)
            ],
            axis=0,
        )
        table = table_ref[SHIFT - shift : SHIFT - shift + WINDOWED, :]
        pieces.append(jnp.dot(stacked, table, preferred_element_type=jnp.float32) * INV_ROOT)
    for bit in (1, 2):
        pieces = [
            pieces[i] + pieces[i ^ bit] if i & bit == 0 else pieces[i ^ bit] - pieces[i]
            for i in range(4)
        ]
    for half in range(2):
        carried = None
        for place in range(4):
            upper, lower = pieces[place][:rows], pieces[place][rows:]
            value = upper + lower if half == 0 else upper - lower
            shift = place * PIECE % 128
            first = half * pair + place * PIECE - shift
            if shift:
                value = pltpu.roll(value, shift, 1)
                value = jnp.concatenate([value[:, :128] + carried, value[:, 128:]], axis=1)
            keep = WINDOWED if place == 3 else WINDOWED - 128
            out_ref[:, first : first + keep] = value[:, :keep].astype(jnp.bfloat16)
            carried = value[:, keep:]


def mix_hidden(hidden, *earlier):
    rows, width = hidden.shape
    step = 256
    return pl.pallas_call(
        mix_kernel,
        grid=(rows // step,),
        in_specs=[
            pl.BlockSpec((step, width), lambda i: (i, 0)),
            pl.BlockSpec((WINDOWED + SHIFT, WINDOWED), lambda i: (0, 0)),
        ]
        + [ANYWHERE] * len(earlier),
        out_specs=pl.BlockSpec((step, width), lambda i: (i, 0)),
        out_shape=jax.ShapeDtypeStruct((rows, width), jnp.bfloat16),
        compiler_params=pltpu.CompilerParams(vmem_limit_bytes=56 << 20),
        cost_estimate=cost(16),
        name="mix",
    )(hidden, mix_tables(), *earlier)


def dequant_kernel(first, half_ref, codes_ref, scales_ref, spread_ref, *refs):
    out_ref, wide = refs[-2:]
    step = codes_ref.shape[0]

    @pl.when(pl.program_id(0) == 0)
    def _():
        scales = scales_ref[:, first : first + wide.shape[0]].astype(jnp.bfloat16)
        wide[...] = lax.dot_general(
            scales, spread_ref[...], (((0,), (0,)), ((), ())), preferred_element_type=jnp.float32
        )

    rows = pl.ds(pl.multiple_of(pl.program_id(0) * step, step), step)
    out_ref[...] = ((codes_ref[...] - 8).astype(jnp.float32) * wide[rows, :]).astype(jnp.bfloat16)


def dequant(half_id, codes, scales, first, size, earlier=()):
    width = codes.shape[1] // 2
    step = next(rows for rows in (112, 96, 48) if first % rows == size % rows == 0)
    groups = scales.shape[0]
    spread = np.repeat(np.eye(groups, dtype=np.float32) * CODE_STEP, GROUP, axis=1)
    return pl.pallas_call(
        lambda *refs: dequant_kernel(first, *refs),
        grid_spec=pltpu.PrefetchScalarGridSpec(
            num_scalar_prefetch=1,
            grid=(size // step,),
            in_specs=[
                pl.BlockSpec((step, width), lambda i, half: (first // step + i, half[0])),
                pl.BlockSpec(scales.shape, lambda i, half: (0, 0)),
                pl.BlockSpec((groups, width), lambda i, half: (0, half[0])),
            ]
            + [ANYWHERE] * len(earlier),
            out_specs=pl.BlockSpec((step, width), lambda i, half: (i, 0)),
            scratch_shapes=[pltpu.VMEM((size, width), jnp.float32)],
        ),
        out_shape=jax.ShapeDtypeStruct((size, width), jnp.bfloat16),
        cost_estimate=cost(3),
        name="decode",
    )(half_id, codes, scales, jnp.asarray(spread, dtype=jnp.bfloat16), *earlier)


def level_kernel(sign_ref, own_ref, partner_ref, *refs):
    sign = sign_ref[0].astype(jnp.float32).astype(jnp.bfloat16)
    out_refs = refs[-1:]
    out_refs[0][...] = own_ref[...] * sign + partner_ref[...]


def level_step(value, bit, earlier=()):
    partner = flipped(value, "tp", bit)
    sign = jnp.where(lax.axis_index("tp") & bit == 0, 1, -1).reshape(1)
    size, width = value.shape
    step = next(rows for rows in (112, 96, 80, 64, 48) if size % rows == 0)
    spec = pl.BlockSpec((step, width), lambda i, sign: (i, 0))
    return pl.pallas_call(
        level_kernel,
        grid_spec=pltpu.PrefetchScalarGridSpec(
            num_scalar_prefetch=1,
            grid=(size // step,),
            in_specs=[spec, spec] + [ANYWHERE] * len(earlier),
            out_specs=spec,
        ),
        out_shape=jax.ShapeDtypeStruct(value.shape, jnp.bfloat16),
        cost_estimate=cost(3),
        name="level",
    )(sign, value, partner, *earlier)


def gate_kernel(*refs):
    pass


def gate(value, *earlier):
    return pl.pallas_call(
        gate_kernel,
        in_specs=[ANYWHERE] * (1 + len(earlier)),
        out_specs=ANYWHERE,
        out_shape=jax.ShapeDtypeStruct(value.shape, value.dtype),
        input_output_aliases={0: 0},
        cost_estimate=cost(0),
        name="gate",
    )(value, *earlier)


def project_kernel(chunks, flips, place_ref, *refs):
    count = len(flips)
    row_refs, attn_refs, side_ref = refs[:count], refs[count : 2 * count], refs[2 * count]
    weights = refs[2 * count + 1 : 2 * count + 1 + 2 * len(chunks)]
    out_ref, total, attn, out_side, arrived = refs[-5:]
    step = pl.program_id(0)
    steps = pl.num_programs(0)
    rows = row_refs[0].shape[0]
    shards = out_ref.shape[0]
    kept = rows // shards

    def add(parts, sources, first):
        part = jnp.concatenate(parts, axis=0)
        for place, ref in enumerate(sources):
            lanes = slice(place * rows, (place + 1) * rows)
            value = lax.dot_general(part, ref[...], NT, preferred_element_type=jnp.float32)
            total[:, lanes] = value if first else total[:, lanes] + value

    def fetches():
        yield pltpu.make_async_copy(side_ref, out_side, arrived.at[count])
        for place, flip in enumerate(flips):
            block = 0 if flip is None else place_ref[1] ^ flip
            source = attn_refs[place].at[pl.ds(pl.multiple_of(block * rows, rows), rows), :]
            yield pltpu.make_async_copy(source, attn.at[place], arrived.at[place])

    @pl.when(step == 0)
    def _():
        for fetch in fetches():
            fetch.start()
        add([ref[...] for ref in weights[0::2]], row_refs, True)

    @pl.when((step > 0) & (step < steps // 2))
    def _():
        add([ref[...] for ref in weights[0::2]], row_refs, False)

    @pl.when(step >= steps // 2)
    def _():
        add([ref[...] for ref in weights[1::2]], row_refs, False)

    @pl.when(step == steps - 1)
    def _():
        for fetch in fetches():
            fetch.wait()
        side = [out_side[first : first + size, :] for first, size in chunks]
        add(side, [attn.at[place] for place in range(count)], False)
        for shard in range(shards):
            for place in range(count):
                first = place * rows + shard * kept
                out_ref[shard, :, place * kept : (place + 1) * kept] = total[
                    :, first : first + kept
                ].astype(jnp.bfloat16)


def project(place, shards, row_parts, attn_parts, out_side, weights, chunks, earlier=()):
    count = len(row_parts)
    rows, width = row_parts[0].shape
    steps = 6
    depth = width // steps
    last = steps // 2 - 1
    columns = sum(size for _, size in chunks)
    weight_specs = []
    for _, size in chunks:
        weight_specs += [
            pl.BlockSpec((size, depth), lambda i, h: (0, jnp.minimum(i, last))),
            pl.BlockSpec((size, depth), lambda i, h: (0, jnp.maximum(i - last - 1, 0))),
        ]
    row_spec = pl.BlockSpec((rows, depth), lambda i, h: (0, lax.rem(i + h[0] * (last + 1), steps)))

    shape = (shards, columns, count * rows // shards)
    return pl.pallas_call(
        lambda *refs: project_kernel(chunks, [flip for _, flip in attn_parts], *refs),
        grid_spec=pltpu.PrefetchScalarGridSpec(
            num_scalar_prefetch=1,
            grid=(steps,),
            in_specs=[row_spec] * count
            + [ANYWHERE] * (count + 1)
            + weight_specs
            + [ANYWHERE] * len(earlier),
            out_specs=pl.BlockSpec(shape, lambda i, h: (0, 0, 0)),
            scratch_shapes=[
                pltpu.VMEM((columns, count * rows), jnp.float32),
                pltpu.VMEM((count, rows, out_side.shape[1]), jnp.bfloat16),
                pltpu.VMEM(out_side.shape, jnp.bfloat16),
                pltpu.SemaphoreType.DMA((count + 1,)),
            ],
        ),
        out_shape=jax.ShapeDtypeStruct(shape, jnp.bfloat16),
        compiler_params=pltpu.CompilerParams(vmem_limit_bytes=56 << 20),
        cost_estimate=cost(10),
        name="project",
    )(place, *row_parts, *[part for part, _ in attn_parts], out_side, *weights, *earlier)


def turned(head, cosine, signed_sine):
    head = head.astype(jnp.float32)
    return (head * cosine + pltpu.roll(head, HD // 2, 1) * signed_sine).astype(jnp.bfloat16)


def attend_kernel(place_ref, query_ref, cosine_ref, sine_ref, *refs):
    blocks, out_ref = refs[:16], refs[-1]
    rows = query_ref.shape[0]
    half = rows // 2
    heads = query_ref.shape[1] // HD
    key0, value0 = blocks[:2]
    keys = [turned(key0[...], cosine_ref[...], sine_ref[...])]
    values = [value0[...]]
    for block in (1, 2):
        key, value, cosine, sine, cached_key, cached_value = blocks[6 * block - 4 : 6 * block + 2]
        inside = place_ref[0] >= block
        keys.append(
            jnp.where(inside, turned(key[...], cosine[...], sine[...]), cached_key[...])
        )
        values.append(jnp.where(inside, value[...], cached_value[...]))
    for part in range(2):
        low = part * half
        here = slice(low, low + half)
        own = slice(0, low + half)
        old = slice(low, rows)
        query = jnp.concatenate(
            [
                turned(
                    query_ref[here, head * HD : (head + 1) * HD],
                    cosine_ref[here, :],
                    sine_ref[here, :],
                )
                for head in range(heads)
            ],
            axis=0,
        )

        def score(block):
            return lax.dot_general(query, block, NT, preferred_element_type=jnp.float32)

        def places(count, first):
            query_at = lax.broadcasted_iota(jnp.int32, (heads, half, count), 1) + low
            key_at = lax.broadcasted_iota(jnp.int32, (heads, half, count), 2) + first
            shape = (heads * half, count)
            return query_at.reshape(shape), key_at.reshape(shape)

        score0, score1, score2 = score(keys[0][own, :]), score(keys[1]), score(keys[2][old, :])
        query_at, key_at = places(low + half, 0)
        score0 = jnp.where(key_at <= query_at, score0, -jnp.inf)
        query_at, key_at = places(rows - low, low)
        score2 = jnp.where(key_at > query_at, score2, -jnp.inf)
        top = jnp.maximum(
            jnp.max(score0, axis=1, keepdims=True),
            jnp.maximum(
                jnp.max(score1, axis=1, keepdims=True), jnp.max(score2, axis=1, keepdims=True)
            ),
        )
        top = top * EXPONENT
        total = jnp.zeros((heads * half, 2 * HD), jnp.float32)
        for scores, block in (
            (score0, values[0][own, :]),
            (score1, values[1]),
            (score2, values[2][old, :]),
        ):
            weight = jnp.exp2(scores * EXPONENT - top).astype(jnp.bfloat16)
            block = jnp.concatenate([block, jnp.ones_like(block)], axis=1)
            total += jnp.dot(weight, block, preferred_element_type=jnp.float32)
        total = (total[:, :HD] / total[:, HD:]).astype(jnp.bfloat16)
        for head in range(heads):
            out_ref[here, head * HD : (head + 1) * HD] = total[head * half : (head + 1) * half]


def attend(places, queries, cosine, signed_sine, all_pairs, ordered, earlier, weight):
    rows = ordered.shape[0] // 2
    width = queries.shape[1]
    kv_heads = all_pairs.shape[1] // (2 * HD)
    wide = width // kv_heads
    gathered = queries.shape[0] > rows

    def pair_specs(row):
        return [
            pl.BlockSpec((rows, HD), lambda i, p: (row(p[0]), i)),
            pl.BlockSpec((rows, HD), lambda i, p: (row(p[0]), kv_heads + i)),
        ]

    def table_specs(row):
        return [pl.BlockSpec((rows, HD), lambda i, p: (row(p[0]), 0))] * 2

    def back(block):
        return lambda place: jnp.maximum(place - block, 0)

    specs = [pl.BlockSpec((rows, wide), lambda i, p: (p[0] if gathered else 0, i))]
    specs += table_specs(back(0)) + pair_specs(back(0))
    operands = [queries, cosine, signed_sine, all_pairs, all_pairs]
    for block in (1, 2):
        specs += pair_specs(back(block)) + table_specs(back(block))
        specs += pair_specs(lambda place, block=block: jnp.minimum(place + 2 - block, 1))
        operands += [all_pairs, all_pairs, cosine, signed_sine, ordered, ordered]
    return pl.pallas_call(
        attend_kernel,
        grid_spec=pltpu.PrefetchScalarGridSpec(
            num_scalar_prefetch=1,
            grid=(kv_heads,),
            in_specs=specs + [ANYWHERE] * len(earlier),
            out_specs=pl.BlockSpec((rows, wide), lambda i, p: (0, i)),
        ),
        out_shape=jax.ShapeDtypeStruct((rows, width), jnp.bfloat16),
        compiler_params=pltpu.CompilerParams(vmem_limit_bytes=56 << 20),
        cost_estimate=cost(weight),
        name="attend",
    )(places, *operands, *earlier)


def flipped(value, axis, bit):
    return lax.ppermute(value, axis, [(i, i ^ bit) for i in range(lax.axis_size(axis))])


def planned(
    queries, key_value, window_cache, span_start, hidden, down_codes, down_scales, out_weight
):
    half_id = lax.axis_index("group").reshape(1)
    seq_index = lax.axis_index("seq")
    core = seq_index & 1
    side = seq_index >> 1
    tok_rows = queries.shape[0]

    pairs = key_value.reshape(tok_rows, -1)
    all_pairs = lax.all_gather(pairs, "seq", axis=0, tiled=True)

    def both_cores(value):
        return [value, flipped(value, "seq", 1)]

    codes = down_codes.T
    out_own = out_weight.T
    (piece_a, piece_c), (piece_b, piece_d) = EARLY, LATE
    piece_a = dequant(half_id, codes, down_scales, *piece_a)
    piece_c = dequant(half_id, codes, down_scales, *piece_c, (piece_a, pairs))
    near_queries = flipped(queries, "seq", 1)
    piece_b = dequant(half_id, codes, down_scales, *piece_b, (piece_c, near_queries))
    near_hidden = flipped(hidden, "seq", 1)
    rotated = mix_hidden(hidden, piece_b)

    first_pos = gate(span_start, piece_b)[0]
    span = tok_rows * lax.axis_size("seq")
    positions = first_pos + jnp.arange(span, dtype=jnp.int32)
    inv_freq = ROPE_BASE ** (-(2.0 * jnp.arange(HD // 2, dtype=jnp.float32)) / HD)
    angles = positions.astype(jnp.float32)[:, None] * inv_freq[None, :]
    cosine, sine = jnp.cos(angles), jnp.sin(angles)
    cosine = jnp.concatenate([cosine, cosine], axis=1)
    signed_sine = jnp.concatenate([-sine, sine], axis=1)
    cache = window_cache.reshape(WINDOW, -1)
    doubled = jnp.concatenate([cache, cache], axis=0)
    ordered = lax.dynamic_slice_in_dim(doubled, first_pos % WINDOW, WINDOW, 0)


    piece_a = level_step(piece_a, 2, (rotated, ordered, cosine, signed_sine))
    piece_c = level_step(piece_c, 1, (piece_a,))


    def attended_by(flip, rows, earlier, weight):
        places = (seq_index ^ flip).reshape(1)
        return attend(places, rows, cosine, signed_sine, all_pairs, ordered, earlier, weight)

    attended = attended_by(0, queries, (piece_c,), 13)
    all_attended = lax.all_gather(attended, "seq", axis=0, tiled=True)
    late_d = dequant(half_id, codes, down_scales, *LATE[1], (attended,))
    own_rows = [rotated, mix_hidden(near_hidden, late_d)]
    piece_b = level_step(piece_b, 2, (piece_c, own_rows[1]))
    piece_a = level_step(piece_a, 1, (piece_b,))
    across_a = flipped(piece_a, "group", 1)
    near_attended = attended_by(1, near_queries, (piece_a,), 0)
    piece_c = level_step(piece_c, 2, (near_attended,))
    across_c = flipped(piece_c, "group", 1)
    piece_d = level_step(late_d, 1, (piece_c,))
    piece_b = level_step(piece_b, 1, (piece_d, across_a))
    across_b = flipped(piece_b, "group", 1)
    place = jnp.stack([half_id[0], seq_index])
    own_attn = [(attended, None), (near_attended, None)]
    far_attn = [(all_attended, 2), (all_attended, 3)]
    shards = lax.axis_size("tp")

    def reduced(rows, attn, weights, chunks, earlier=(), after=()):
        partial = project(place, shards, rows, attn, out_own, weights, chunks, earlier)
        if after:
            partial = gate(partial, *after)
        return lax.psum_scatter(partial, "tp", scatter_dimension=0, tiled=True)[0], partial

    early = [piece_a, across_a, piece_c, across_c]
    own_early, own_done = reduced(own_rows, own_attn, early, EARLY, (piece_b,))
    piece_d = level_step(piece_d, 2, (piece_b, own_done))
    across_d = flipped(piece_d, "group", 1)
    far_rows = both_cores(gate(flipped(rotated, "seq", 2), piece_d,across_b))
    late = [piece_b, across_b, piece_d, across_d]
    far_early, far_done = reduced(far_rows, far_attn, early, EARLY, (piece_d,))
    all_late, _ = reduced(
        own_rows + far_rows, own_attn + far_attn, late, LATE, (far_done, own_early), (far_early,)
    )
    kept = tok_rows // shards

    def handed_out(sums):
        strips = [sums[:, i * kept : (i + 1) * kept] for i in range(4)]
        return strips[:1] + [flipped(strips[i], "seq", i) for i in (1, 2, 3)]

    early_strips = handed_out(jnp.concatenate([own_early, far_early], axis=1))
    late_strips = handed_out(all_late)
    wide, rest = WIDE, HALF - WIDE
    strips = [
        jnp.concatenate([x[:wide], y[:rest], x[wide:], y[rest:]], axis=0)
        for x, y in zip(early_strips, late_strips)
    ]
    strips = [jnp.where(core == 0, strips[i], strips[i ^ 1]) for i in range(4)]
    strips = [jnp.where(side == 0, strips[i], strips[i ^ 2]) for i in range(4)]
    return jnp.concatenate(strips, axis=0).T


def solution(mesh):
    return jax.shard_map(
        planned if fits(mesh) else per_device,
        mesh=mesh,
        in_specs=(
            P(("group", "seq"), "tp"),
            P(("group", "seq"), None, "tp"),
            P("group", None, "tp"),
            P("group"),
            P(("group", "seq"), "tp"),
            P("tp", "seq"),
            P("tp", "seq"),
            P("tp", "seq"),
        ),
        out_specs=P(("group", "seq", "tp"), None),
        check_vma=False,
    )
```
